128 devices in a mesh: dp: 64 (over z, y_hi, x, core), expert: 2 (over y_lo).
Axes of the slice: x: 4, y: 4 (y_hi: 2, y_lo: 2; y = y_hi * 2 + y_lo), z: 4, core: 2. Of those that a mesh axis runs over, the one named last changes fastest.
Arguments:
- tokens: bfloat16 [256, 64, 1536], P(('dp', 'expert')), may hold values from -6 to 6
- segment_ids: int32 [256, 64], P(('dp', 'expert')), may hold values from 0 to 7, never falling along the last dimension, each value on 1 to 16 neighbouring positions
- routes: int32 [256, 64, 8], P(('dp', 'expert')), may hold values from 0 to 15, all different within a row
- cotangent: bfloat16 [256, 64, 1536], P(('dp', 'expert')), may hold values from -6 to 6
- attn_gain: bfloat16 [1536], P(('dp', 'expert')), may hold values from 0.5 to 1.5
- query_weight: bfloat16 [1536, 1536], P(('dp', 'expert')), may hold values from -0.15625 to 0.15625
- key_weight: bfloat16 [1536, 512], P(('dp', 'expert')), may hold values from -0.15625 to 0.15625
- value_weight: bfloat16 [1536, 512], P(('dp', 'expert')), may hold values from -0.15625 to 0.15625
- output_weight: bfloat16 [1536, 1536], P(('dp', 'expert')), may hold values from -0.625 to 0.625
- expert_gain: bfloat16 [1536], P(('dp', 'expert')), may hold values from 0.5 to 1.5
- router_weight: bfloat16 [1536, 16], P(('dp', 'expert')), may hold values from -0.078125 to 0.078125
- expert_in: bfloat16 [16, 1536, 1024], P('expert', 'dp'), may hold values from -0.15625 to 0.15625
- expert_out: bfloat16 [16, 512, 1536], P('expert', 'dp'), may hold values from -1 to 1
Outputs:
- block_out: bfloat16 [256, 64, 1536], P(('dp', 'expert'))
- token_grad: bfloat16 [256, 64, 1536], P(('dp', 'expert'))
- attn_gain_grad: float32 [1536], P(('dp', 'expert'))
- query_weight_grad: float32 [1536, 1536], P(('dp', 'expert'))
- key_weight_grad: float32 [1536, 512], P(('dp', 'expert'))
- value_weight_grad: float32 [1536, 512], P(('dp', 'expert'))
- output_weight_grad: float32 [1536, 1536], P(('dp', 'expert'))
- expert_gain_grad: float32 [1536], P(('dp', 'expert'))
- router_weight_grad: float32 [1536, 16], P(('dp', 'expert'))
- expert_in_grad: float32 [16, 1536, 1024], P('expert', 'dp')
- expert_out_grad: float32 [16, 512, 1536], P('expert', 'dp')
The draws below stay inside these ranges and needn't reach their ends.
Inputs may be any that keep to these rules, and one draw needn't show every extreme that they name: `segment_ids`: positions of segment 0 (padding) come first in a row, then documents 1, 2, ... in order; each segment spans 1 to 16 positions. `routes`: each token names 8 different experts; every expert is named by some token.
All inputs are finite; a program needn't handle non-finite values.
Results may differ from the reference program's by a relative error of at most 0.015.
Values may be sent and summed in bfloat16 or wider, within the bound.
No kernel may reach another device: no remote copies, remote signals or barrier semaphores. Data moves between devices by JAX's collectives and lax.ppermute only.
A program may use at most 320 MiB of HBM per device.

```python
import math
import jax
import jax.numpy as jnp
import numpy as np
from jax import lax

D = 1536
Q_HEADS = 24
KV_HEADS = 8
HEAD_DIM = 64
F = 512
TOPK = 8
EXPERTS = 16
SEQ = 64
SEQS = 256
CAP = 32


def shard_levels(own_key, shape, cuts, low, high):
    loudness, own = 1.0, jax.random.fold_in(own_key, 6)
    for position, blocks in cuts:
        steps = jnp.exp(jax.random.uniform(jax.random.fold_in(own, position), (blocks,), jnp.float32, low / len(cuts), high / len(cuts)))
        loudness = loudness * jnp.repeat(steps, shape[position] // blocks).reshape([-1 if axis == position else 1 for axis in range(len(shape))])
    return loudness


def picks_of(own_key, rows, amount, top, lift):
    sequence = jax.random.permutation(jax.random.fold_in(own_key, 1), amount)
    pull = sequence
    for power in range(3):
        pull = pull * pull // amount
    pull = pull * lift // amount
    chance = jax.random.randint(jax.random.fold_in(own_key, 2), (rows, amount), 0, 4096) + pull
    sure = jax.random.permutation(jax.random.fold_in(own_key, 3), rows)[jnp.arange(amount) % rows]
    chance = jnp.where(jnp.arange(rows)[:, None] == sure[None, :], 1 << 14, chance)
    merit = chance * amount + jnp.arange(amount)
    return lax.top_k(merit.astype(jnp.int32), top)[1].astype(jnp.int32)


def split_up(number_of, total, reach, lean):
    portions = [(1 << 20) // math.isqrt(rank ** lean) + 1 for rank in range(2, number_of + 1)]
    spare, given = total - reach - (number_of - 1), [1] * (number_of - 1)
    while spare > 0:
        free = [i for i in range(number_of - 1) if given[i] < reach]
        pool, budget = sum([portions[i] for i in free]), spare
        for i in free:
            addition = min(reach - given[i], max(1, budget * portions[i] // pool), spare)
            given[i] = given[i] + addition
            spare = spare - addition
    return np.array([reach] + given)


def uneven(rng, number_of, total, most, slope):
    if number_of == 2:
        one = jax.random.randint(rng, (), max(1, total - most), min(most, total - 1) + 1)
        return jnp.stack([one, total - one])
    sizes = jnp.asarray(split_up(number_of, total, most, slope), jnp.int32)
    twos = (number_of - 1) // 2
    giver, receiver = sizes[1:1 + 2 * twos:2], sizes[2:2 + 2 * twos:2]
    slack = jnp.minimum(giver - 1, most - receiver)
    passed = jax.random.randint(jax.random.fold_in(rng, 1), (twos,), 0, 1 << 20) % (slack + 1)
    sizes = sizes.at[1:1 + 2 * twos:2].set(giver - passed).at[2:2 + 2 * twos:2].set(receiver + passed)
    return sizes[jax.random.permutation(jax.random.fold_in(rng, 2), number_of)]


def centred(key, extent, spread, limit, shards=(), kind=jnp.bfloat16):
    drawn = spread * jax.random.normal(key, extent, jnp.float32)
    if shards:
        drawn = drawn * shard_levels(key, extent, shards, -0.22, 0.18)
    return jnp.clip(drawn, -limit, limit).astype(kind)


def setup_inputs(seed: int = 0) -> dict:
    splits = jax.random.split(jax.random.key(seed), 14)
    return {
        "tokens": centred(splits[0], (SEQS, SEQ, D), 1.0, 6.0, ((0, 128),)),
        "segment_ids": jax.vmap(lambda own: jnp.searchsorted(jnp.cumsum(uneven(own, 8, SEQ, SEQ // 4, 1)), jnp.arange(SEQ), side="right"))(jax.random.split(splits[1], SEQS)).reshape((SEQS, SEQ)).astype(jnp.int32),
        "routes": picks_of(splits[2], SEQS * SEQ, EXPERTS, TOPK, 4096).reshape((SEQS, SEQ, TOPK)),
        "cotangent": centred(splits[3], (SEQS, SEQ, D), 1.0, 6.0, ((0, 128),)),
        "attn_gain": jnp.clip(1.0 + 0.1 * jax.random.normal(splits[4], (D,), jnp.float32), 0.5, 1.5).astype(jnp.bfloat16),
        "query_weight": centred(splits[5], (D, Q_HEADS * HEAD_DIM), D ** -0.5, 0.15625, ((0, 128),)),
        "key_weight": centred(splits[6], (D, KV_HEADS * HEAD_DIM), D ** -0.5, 0.15625, ((0, 128),)),
        "value_weight": centred(splits[7], (D, KV_HEADS * HEAD_DIM), D ** -0.5, 0.15625, ((0, 128),)),
        "output_weight": centred(splits[8], (Q_HEADS * HEAD_DIM, D), (Q_HEADS * HEAD_DIM // 16) ** -0.5, 0.625, ((0, 128),)),
        "expert_gain": jnp.clip(1.0 + 0.1 * jax.random.normal(splits[9], (D,), jnp.float32), 0.5, 1.5).astype(jnp.bfloat16),
        "router_weight": centred(splits[10], (D, EXPERTS), (4 * D) ** -0.5, 0.078125, ((0, 128),)),
        "expert_in": centred(splits[11], (EXPERTS, D, 2 * F), D ** -0.5, 0.15625, ((0, 2), (1, 64))),
        "expert_out": centred(splits[12], (EXPERTS, F, D), (F // 16) ** -0.5, 1.0, ((0, 2), (1, 64))),
    }


@jax.custom_vjp
def low(v):
    return lax.optimization_barrier(v.astype(jnp.bfloat16)).astype(jnp.float32)

@jax.custom_vjp
def low_back(v):
    return v

def low_keep(v):
    return (low(v), None)

def low_pass(kept, grad):
    return (grad,)

def back_keep(v):
    return (v, None)

def back_low(kept, grad):
    return (low(grad),)
low.defvjp(low_keep, low_pass)
low_back.defvjp(back_keep, back_low)
HIGHEST = lax.Precision.HIGHEST
norm_eps = 1e-05

def rms_norm(values, gain_vec):
    return values * lax.rsqrt(lax.optimization_barrier(jnp.mean(values * values, axis=-1, keepdims=True)) + norm_eps) * gain_vec

def rotary_tables(seq_len):
    positions = jnp.arange(seq_len, dtype=jnp.float32)
    inverse_freq = 10000.0 ** (-jnp.arange(HEAD_DIM // 2, dtype=jnp.float32) * 2.0 / HEAD_DIM)
    angles = positions[:, None] * inverse_freq[None, :]
    return (jnp.cos(angles)[:, None, :], jnp.sin(angles)[:, None, :])

def rotate(values, cosine, sine_vals):
    first_half = values[..., :HEAD_DIM // 2]
    second_half = values[..., HEAD_DIM // 2:]
    return jnp.concatenate([first_half * cosine - second_half * sine_vals, second_half * cosine + first_half * sine_vals], axis=-1)

def slot_tables(segment_row, route_row, experts_all, capacity):
    valid_tok = segment_row > 0
    flat_routes = route_row.reshape(-1).astype(jnp.int32)
    live_route = jnp.repeat(valid_tok, route_row.shape[1])
    route_onehot = (flat_routes[:, None] == jnp.arange(experts_all, dtype=jnp.int32)[None, :]) & live_route[:, None]
    counts = jnp.cumsum(route_onehot.astype(jnp.int32), axis=0)
    ranking = lax.optimization_barrier(jnp.sum(jnp.where(route_onehot, counts - 1, 0), axis=1)).astype(jnp.int32)
    kept_mask = live_route & (ranking < capacity)
    dest_slot = jnp.where(kept_mask, flat_routes * capacity + ranking, experts_all * capacity).astype(jnp.int32)
    route_ids = jnp.arange(flat_routes.shape[0], dtype=jnp.int32)
    slot_route = jnp.zeros((experts_all * capacity,), jnp.int32).at[dest_slot].set(route_ids, mode='drop')
    slot_filled = jnp.zeros((experts_all * capacity,), jnp.bool_).at[dest_slot].set(True, mode='drop')
    return (kept_mask, dest_slot, slot_route, slot_filled)

def layer_forward(inputs, attn_gain, query_weight, key_weight, value_weight, output_weight, expert_gain, router_weight, expert_in, expert_out, segment_row, route_row):
    seq_len = inputs.shape[0]
    group_heads = Q_HEADS // KV_HEADS
    cosine, sine_vals = rotary_tables(seq_len)
    normed = low(rms_norm(inputs, attn_gain))
    queries = low_back(jnp.dot(normed, query_weight, precision=HIGHEST)).reshape(seq_len, Q_HEADS, HEAD_DIM)
    queries = low(rotate(queries, cosine, sine_vals)).reshape(seq_len, KV_HEADS, group_heads, HEAD_DIM)
    keys_raw = low_back(jnp.dot(normed, key_weight, precision=HIGHEST)).reshape(seq_len, KV_HEADS, HEAD_DIM)
    keys_rot = low(rotate(keys_raw, cosine, sine_vals))
    values = low(low_back(jnp.dot(normed, value_weight, precision=HIGHEST))).reshape(seq_len, KV_HEADS, HEAD_DIM)
    scores = low_back(jnp.einsum('sjgd,tjd->jgst', queries, keys_rot, precision=HIGHEST) * HEAD_DIM ** (-0.5))
    positions = jnp.arange(seq_len)
    allowed = (segment_row[:, None] == segment_row[None, :]) & (positions[None, :] <= positions[:, None])
    scores = jnp.where(allowed, scores, -1e+30)
    row_top = lax.optimization_barrier(jnp.max(scores, axis=-1, keepdims=True))
    expo_vals = jnp.exp(scores - row_top)
    attn_probs = expo_vals / lax.optimization_barrier(jnp.sum(expo_vals, axis=-1, keepdims=True))
    mixed_heads = jnp.einsum('jgst,tjd->sjgd', low(attn_probs), values, precision=HIGHEST)
    mixed_heads = low(low_back(mixed_heads)).reshape(seq_len, Q_HEADS * HEAD_DIM)
    attn_out = low_back(jnp.dot(mixed_heads, output_weight, precision=HIGHEST))
    residual = inputs + attn_out
    normed_two = low(rms_norm(residual, expert_gain))
    logits = low_back(jnp.dot(normed_two, router_weight, precision=HIGHEST))
    chosen = jnp.take_along_axis(logits, route_row, axis=1)
    chosen_exp = jnp.exp(chosen - lax.optimization_barrier(jnp.max(chosen, axis=1, keepdims=True)))
    gate_vals = chosen_exp / lax.optimization_barrier(jnp.sum(chosen_exp, axis=1, keepdims=True))
    kept_mask, dest_slot, slot_route, slot_filled = slot_tables(segment_row, route_row, EXPERTS, CAP)
    slot_token = slot_route // TOPK
    dispatched = low_back(jnp.take(normed_two, slot_token, axis=0) * slot_filled.astype(jnp.float32)[:, None])
    dispatched = dispatched.reshape(EXPERTS, CAP, D)
    gate_up = low_back(jnp.einsum('ecd,edf->ecf', dispatched, expert_in, precision=HIGHEST))
    gate_part = gate_up[..., :F]
    hidden = low(gate_part * jax.nn.sigmoid(gate_part) * gate_up[..., F:])
    expert_rows = low(low_back(jnp.einsum('ecf,efd->ecd', hidden, expert_out, precision=HIGHEST))).reshape(EXPERTS * CAP, D)
    safe_slot = jnp.minimum(dest_slot, EXPERTS * CAP - 1)
    route_rows = jnp.take(expert_rows, safe_slot, axis=0).reshape(seq_len, TOPK, D)
    weights_kept = gate_vals * kept_mask.reshape(seq_len, TOPK).astype(jnp.float32)
    mixture = jnp.einsum('sk,skd->sd', weights_kept, route_rows, precision=HIGHEST)
    valid_col = (segment_row > 0).astype(jnp.float32)[:, None]
    return (residual + mixture) * valid_col

def reference(tokens, segment_ids, routes, cotangent, attn_gain, query_weight, key_weight, value_weight, output_weight, expert_gain, router_weight, expert_in, expert_out):
    weights = tuple((tensor.astype(jnp.float32) for tensor in (attn_gain, query_weight, key_weight, value_weight, output_weight, expert_gain, router_weight, expert_in, expert_out)))
    group_size = math.gcd(SEQS, max(1, 4096 // SEQ))
    steps_count = SEQS // group_size

    def regroup(array):
        return array.reshape((steps_count, group_size) + array.shape[1:])

    def one_group(totals, blocks):
        token_blk, segment_blk, route_blk, cot_blk = blocks

        def whole_block(inputs_f, *params):

            def single(inputs_row, segment_row, route_row):
                return layer_forward(inputs_row, *params, segment_row, route_row)
            return jax.vmap(single)(inputs_f, segment_blk, route_blk)
        outputs, pullback = jax.vjp(whole_block, token_blk.astype(jnp.float32), *weights)
        gradients = pullback(cot_blk.astype(jnp.float32))
        totals = tuple((total_item + grad_item for total_item, grad_item in zip(totals, gradients[1:])))
        return (totals, (outputs.astype(jnp.bfloat16), gradients[0].astype(jnp.bfloat16)))
    zero_totals = tuple((jnp.zeros_like(tensor) for tensor in weights))
    totals, stacked = lax.scan(one_group, zero_totals, (regroup(tokens), regroup(segment_ids), regroup(routes), regroup(cotangent)))
    block_out = stacked[0].reshape(SEQS, SEQ, D)
    token_grad = stacked[1].reshape(SEQS, SEQ, D)
    return (block_out, token_grad, totals[0], totals[1], totals[2], totals[3], totals[4], totals[5], totals[6], totals[7], totals[8])
```

```python
import functools

import jax
import jax.numpy as jnp
import numpy as np
from jax import lax
from jax.experimental import pallas as pl
from jax.experimental.pallas import tpu as pltpu
from jax.sharding import Mesh
from jax.sharding import PartitionSpec as P

D = 1536
Q_HEADS = 24
KV_HEADS = 8
HEAD_DIM = 64
F = 512
TOPK = 8
EXPERTS = 16
SEQ = 64
CAP = 32

AX = ("z", "yh", "x", "c", "yl")
DIMS = (4, 2, 4, 2, 2)
EPS = 1e-5
NEG = -1e30
TOK = 128
EXT = 144
QKV = 1280
QKVM = 1408
HQ = 768
HK = 256
bf16 = jnp.bfloat16
f32 = jnp.float32


def coords_list():
    return list(np.ndindex(*DIMS))


def send(value, dz=0, dh=0, dx=0, dc=0, dl=0):
    flat = {pos: i for i, pos in enumerate(coords_list())}
    pairs = [
        (i, flat[(z ^ dz, h ^ dh, x ^ dx, c ^ dc, l ^ dl)])
        for (z, h, x, c, l), i in flat.items()
    ]
    return lax.ppermute(value, AX, pairs)


def dot(a, b):
    return jnp.dot(a, b, preferred_element_type=f32)


def dot_t(a, b):
    return lax.dot_general(a, b, (((1,), (1,)), ((), ())), preferred_element_type=f32)


def t_dot(a, b):
    return lax.dot_general(a, b, (((0,), (0,)), ((), ())), preferred_element_type=f32)


def params(mib=60):
    return pltpu.CompilerParams(vmem_limit_bytes=mib * 2**20)


def rope_tables():
    angle = np.arange(SEQ)[:, None] * (10000.0 ** (-np.arange(32) * 2.0 / 64))[None, :]
    cosine, sine = np.cos(angle), np.sin(angle)
    cos_full = np.concatenate([cosine, cosine] * 2, axis=1)
    sin_full = np.concatenate([-sine, sine] * 2, axis=1)
    return np.tile(cos_full, (4, 1)).astype(np.float32), np.tile(sin_full, (4, 1)).astype(np.float32)


def turn(values, cos_full, sin_full):
    width = values.shape[1]
    lane = lax.broadcasted_iota(jnp.int32, values.shape, 1)
    ahead = pltpu.roll(values, width - 32, 1)
    behind = pltpu.roll(values, 32, 1)
    partner = jnp.where((lane % 64) < 32, ahead, behind)
    copies = width // 128
    cos_wide = jnp.concatenate([cos_full] * copies, axis=1)
    sin_wide = jnp.concatenate([sin_full] * copies, axis=1)
    return values * cos_wide + partner * sin_wide


def allowed_mask(ints):
    row = jnp.broadcast_to(ints[8:9, :], (TOK, TOK))
    col = row.T
    p = lax.broadcasted_iota(jnp.int32, (TOK, TOK), 0)
    t = lax.broadcasted_iota(jnp.int32, (TOK, TOK), 1)
    return (row == col) & (t <= p) & ((p < SEQ) == (t < SEQ))


def piece_copies(pieces, target, sems, z, x):
    copies = []
    for j in range(4):
        for k in range(4):
            for h in range(2):
                start = pl.multiple_of((((z ^ j) * 2 + h) * 4 + (x ^ k)) * 48, 16)
                copies.append(
                    pltpu.make_async_copy(
                        pieces[j * 4 + k].at[pl.ds(48 * h, 48), :],
                        target.at[pl.ds(start, 48), :],
                        sems.at[(j * 4 + k) * 2 + h],
                    )
                )
    return copies


def o_copies(pieces, target, sems, z, x):
    copies = []
    for j in range(4):
        for k in range(4):
            start = pl.multiple_of(((z ^ j) * 4 + (x ^ k)) * 48, 16)
            copies.append(
                pltpu.make_async_copy(
                    pieces[j * 4 + k], target.at[pl.ds(start, 48), :], sems.at[j * 4 + k]
                )
            )
    return copies


def spec_any():
    return pl.BlockSpec(memory_space=pl.ANY)


def spec_vmem():
    return pl.BlockSpec(memory_space=pltpu.VMEM)


def spec_smem():
    return pl.BlockSpec(memory_space=pltpu.SMEM)


def kernel_attn(where, xo, xs, cos_ref, sin_ref, *rest):
    pieces = rest[:16]
    normed_ref, q_ref, k_ref, v_ref, mixed_ref, misc_ref = rest[16:22]
    w, sems = rest[22:]
    copies = piece_copies(pieces, w, sems, where[0], where[2])
    for item in copies:
        item.start()
    xin = jnp.concatenate([xo[:TOK, :], xs[:TOK, :]], axis=0).astype(f32)
    rinv = lax.rsqrt(jnp.mean(xin * xin, axis=1, keepdims=True) + EPS)
    for item in copies:
        item.wait()
    eye = (
        lax.broadcasted_iota(jnp.int32, (128, 128), 0) == lax.broadcasted_iota(jnp.int32, (128, 128), 1)
    ).astype(f32).astype(bf16)
    misc = dot_t(eye, w[:, QKV:])
    misc_ref[...] = misc.astype(bf16)
    normed = (xin * rinv * misc[16:17, :]).astype(bf16)
    normed_ref[...] = normed
    cos_full, sin_full = cos_ref[...], sin_ref[...]
    qf = dot(normed, w[:, :HQ])
    q_ref[...] = turn(qf, cos_full, sin_full).astype(bf16)
    kf = dot(normed, w[:, HQ : HQ + HK])
    k_ref[...] = turn(kf, cos_full, sin_full).astype(bf16)
    v_ref[...] = dot(normed, w[:, HQ + HK : QKV]).astype(bf16)
    for part, src in enumerate((xo, xs)):
        ok = allowed_mask(src[TOK:EXT, :TOK].astype(f32))
        ok3 = jnp.concatenate([ok.astype(f32)] * 3, axis=0) > 0.5
        rows = slice(part * TOK, (part + 1) * TOK)
        for a in range(4):
            keys = k_ref[rows, a * 64 : (a + 1) * 64]
            vals = v_ref[rows, a * 64 : (a + 1) * 64]
            q3 = jnp.concatenate(
                [q_ref[rows, (3 * a + g) * 64 : (3 * a + g + 1) * 64] for g in range(3)], axis=0
            )
            scores = jnp.where(ok3, dot_t(q3, keys) * 0.125, NEG)
            top = jnp.max(scores, axis=1, keepdims=True)
            expo = jnp.exp(scores - top)
            probs = (expo / jnp.sum(expo, axis=1, keepdims=True)).astype(bf16)
            out = dot(probs, vals).astype(bf16)
            for g in range(3):
                mixed_ref[rows, (3 * a + g) * 64 : (3 * a + g + 1) * 64] = out[
                    g * TOK : (g + 1) * TOK, :
                ]


def kernel_oproj(where, mixed_ref, *rest):
    pieces = rest[:16]
    own_ref, sib_ref, w, sems = rest[16:]
    copies = o_copies(pieces, w, sems, where[0], where[2])
    for item in copies:
        item.start()
    for item in copies:
        item.wait()
    out = dot(mixed_ref[...], w[...])
    own_ref[...] = out[:TOK, :]
    sib_ref[...] = out[TOK:, :]


def chosen_gates(misc, n2, ints):
    logits = dot_t(misc, n2)
    expert = lax.broadcasted_iota(jnp.int32, logits.shape, 0).astype(f32)
    hot = jnp.zeros(logits.shape, f32)
    for k in range(TOPK):
        hot = jnp.maximum(hot, (expert == ints[k : k + 1, :]).astype(f32))
    masked = jnp.where(hot > 0.5, logits, NEG)
    expo = jnp.where(hot > 0.5, jnp.exp(masked - jnp.max(masked, axis=0, keepdims=True)), 0.0)
    return expo / jnp.sum(expo, axis=0, keepdims=True)


def kernel_resid(xo, own_ref, recv_ref, misc_ref, resid_ref, n2_ref, gates_ref):
    resid = xo[:TOK, :].astype(f32) + own_ref[...] + recv_ref[...]
    resid_ref[...] = resid
    rinv = lax.rsqrt(jnp.mean(resid * resid, axis=1, keepdims=True) + EPS)
    n2 = (resid * rinv * misc_ref[17:18, :].astype(f32)).astype(bf16)
    n2_ref[...] = n2
    gates_ref[...] = chosen_gates(misc_ref[0:16, :], n2, xo[TOK:EXT, :TOK].astype(f32))


def kernel_expert(where, misc_ref, *rest):
    n2_in = rest[:16]
    gx_in = rest[16:32]
    w_in = rest[32:40]
    dn_own, dn_sib, mix_own, mix_sib = rest[40:44]
    wg_out = rest[44:52]
    (n2, gx, win, wout, disp, dslot, hid, dgu, gate_s, slot_s, hit_s, obuf, mbuf, wg,
     n2_sem, gx_sem, w_sem, o_sem, g_sem) = rest[52:]
    z, h, x, c, l = where[0], where[1], where[2], where[3], where[4]
    me = (l * 8 + x * 2 + c).astype(f32)
    w_copies = []
    for j in range(4):
        for b in range(2):
            m = j * 2 + b
            blk = (z ^ j) * 2 + (h ^ b)
            w_copies.append(
                pltpu.make_async_copy(
                    w_in[m].at[:, pl.ds(0, 1024)],
                    win.at[pl.ds(pl.multiple_of(blk * 192, 64), 192), :],
                    w_sem.at[m * 4],
                )
            )
            for t in range(3):
                w_copies.append(
                    pltpu.make_async_copy(
                        w_in[m].at[pl.ds(64 * t, 64), pl.ds(1024, 512)],
                        wout.at[pl.ds(pl.multiple_of(blk * 64, 64), 64), pl.ds(512 * t, 512)],
                        w_sem.at[m * 4 + 1 + t],
                    )
                )
    n2_copies = [
        pltpu.make_async_copy(n2_in[m], n2.at[pl.ds(TOK * m, TOK), :], n2_sem.at[m]) for m in range(16)
    ]
    gx_copies = [pltpu.make_async_copy(gx_in[m], gx.at[m], gx_sem.at[m]) for m in range(16)]
    for item in gx_copies + n2_copies + w_copies:
        item.start()
    for item in gx_copies + n2_copies:
        item.wait()
    token = lax.broadcasted_iota(jnp.int32, (TOK, TOK), 0)
    after = lax.broadcasted_iota(jnp.int32, (TOK, TOK), 1)
    before = ((token < after) & ((token < SEQ) == (after < SEQ))).astype(f32).astype(bf16)
    router = misc_ref[0:16, :]
    for m in range(16):
        ints = gx[m, TOK:EXT, :TOK].astype(f32)
        gates = chosen_gates(router, n2[TOK * m : TOK * (m + 1), :], ints)
        expert = lax.broadcasted_iota(jnp.int32, gates.shape, 0).astype(f32)
        gate_s[m : m + 1, :] = jnp.sum(jnp.where(expert == me, gates, 0.0), axis=0, keepdims=True)
        hit = jnp.max((ints[0:8, :] == me).astype(f32), axis=0, keepdims=True)
        hit_s[m : m + 1, :] = hit * (ints[8:9, :] > 0.5).astype(f32)
    hit = hit_s[...]
    rank = dot(hit.astype(bf16), before)
    lane = lax.broadcasted_iota(jnp.int32, (16, TOK), 1)
    kept = (hit > 0.5) & (rank < CAP - 0.5)
    slot_s[...] = jnp.where(kept, rank + jnp.where(lane < SEQ, 0.0, 1.0 * CAP), -1.0)
    for item in w_copies:
        item.wait()

    def one_chunk(i, carry):
        slot_iota = lax.broadcasted_iota(jnp.int32, (64, TOK), 0).astype(f32)
        hots, gate_cols = [], []
        rows = pl.ds(pl.multiple_of(i * 256, 256), 256)
        g_parts = []
        for q in range(4):
            m = i * 4 + q
            hot = (slot_iota == slot_s[pl.ds(m, 1), :]).astype(f32)
            gate_col = jnp.sum(hot * gate_s[pl.ds(m, 1), :], axis=1, keepdims=True)
            hot_b = hot.astype(bf16)
            hots.append(hot_b)
            gate_cols.append(gate_col)
            srows = pl.ds(pl.multiple_of(i * 256 + q * 64, 64), 64)
            trows = pl.ds(pl.multiple_of(m * TOK, TOK), TOK)
            disp[srows, :] = dot(hot_b, n2[trows, :]).astype(bf16)
            gsl = dot(hot_b, gx[m, 0:TOK, :])
            g_parts.append(gsl)
            dslot[srows, :] = (gate_col * gsl).astype(bf16)
        gup = dot(disp[rows, :], win[...])
        gate_part, up_part = gup[:, :F], gup[:, F:]
        sig = jax.nn.sigmoid(gate_part)
        hidden = (gate_part * sig * up_part).astype(bf16)
        hid[rows, :] = hidden
        out_rows = dot(hidden, wout[...]).astype(bf16).astype(f32)
        dhid = dot_t(dslot[rows, :], wout[...])
        silu_grad = sig * (1.0 + gate_part * (1.0 - sig))
        dg = jnp.concatenate([dhid * up_part * silu_grad, dhid * gate_part * sig], axis=1).astype(bf16)
        dgu[rows, :] = dg
        din = dot_t(dg, win[...]).astype(bf16)
        for q in range(4):
            part = slice(q * 64, (q + 1) * 64)
            dgate = jnp.sum(g_parts[q] * out_rows[part, :], axis=1, keepdims=True)
            dgate_row = jnp.sum(hots[q].astype(f32) * dgate, axis=0, keepdims=True)
            high = dgate_row.astype(bf16).astype(f32)
            low = dgate_row - high
            line = lax.broadcasted_iota(jnp.int32, (16, TOK), 0)
            extra = jnp.where(line == 2 * c, high, 0.0) + jnp.where(line == 2 * c + 1, low, 0.0)
            obuf[q, 0:TOK, :] = t_dot(hots[q], din[part, :]).astype(bf16)
            obuf[q, TOK:EXT, 0:TOK] = extra.astype(bf16)
            obuf[q, TOK:EXT, TOK:] = jnp.zeros((EXT - TOK, D - TOK), bf16)
            weighted = (gate_cols[q] * out_rows[part, :]).astype(bf16)
            mbuf[q, :, :] = t_dot(hots[q], weighted).astype(bf16)

        @pl.when(i < 2)
        def _():
            c1 = pltpu.make_async_copy(obuf, dn_own.at[pl.ds(i * 4, 4)], o_sem.at[0])
            c2 = pltpu.make_async_copy(mbuf, mix_own.at[pl.ds(i * 4, 4)], o_sem.at[1])
            c1.start()
            c2.start()
            c1.wait()
            c2.wait()

        @pl.when(i >= 2)
        def _():
            c1 = pltpu.make_async_copy(obuf, dn_sib.at[pl.ds(i * 4 - 8, 4)], o_sem.at[0])
            c2 = pltpu.make_async_copy(mbuf, mix_sib.at[pl.ds(i * 4 - 8, 4)], o_sem.at[1])
            c1.start()
            c2.start()
            c1.wait()
            c2.wait()

        return carry

    lax.fori_loop(0, 4, one_chunk, 0)

    def grad_in(b, carry):
        cols = pl.ds(pl.multiple_of(b * 192, 64), 192)
        blk = t_dot(disp[:, cols], dgu[...]) if False else None
        return carry

    for n in range(6):
        wg_rows = slice(n * 256, (n + 1) * 256)
        wg[wg_rows, 0:1024] = t_dot(disp[:, wg_rows], dgu[...]).astype(bf16)
    for n in range(2):
        out_g = t_dot(hid[:, n * 256 : (n + 1) * 256], dslot[...]).astype(bf16)
        for b in range(4):
            blk = n * 4 + b
            for t in range(3):
                wg[blk * 192 + t * 64 : blk * 192 + (t + 1) * 64, 1024:1536] = out_g[
                    b * 64 : (b + 1) * 64, t * 512 : (t + 1) * 512
                ]
    outs = []
    for j in range(4):
        for b in range(2):
            m = j * 2 + b
            blk = (z ^ j) * 2 + (h ^ b)
            outs.append(
                pltpu.make_async_copy(
                    wg.at[pl.ds(pl.multiple_of(blk * 192, 64), 192), :], wg_out[m], g_sem.at[m]
                )
            )
    for item in outs:
        item.start()
    for item in outs:
        item.wait()


def kernel_pair_sum(a_ref, b_ref, *outs):
    for m in range(8):
        outs[m][...] = (a_ref[m].astype(f32) + b_ref[m].astype(f32)).astype(bf16)


def kernel_home(where, gx_ref, resid_ref, n2_ref, gates_ref, misc_ref, *rest):
    pieces = rest[:8]
    dresid_ref, dattn_ref, small_ref, dg_s = rest[8:]
    x, l = where[2], where[4]
    for k in range(4):
        for b in range(2):
            extra = pieces[k * 2 + b][TOK:EXT, 0:TOK].astype(f32)
            first = (l ^ b) * 8 + (x ^ k) * 2
            dg_s[pl.ds(first, 1), :] = extra[0:1, :] + extra[1:2, :]
            dg_s[pl.ds(first + 1, 1), :] = extra[2:3, :] + extra[3:4, :]
    gates = gates_ref[...]
    dgates = dg_s[...]
    dlog = (gates * (dgates - jnp.sum(gates * dgates, axis=0, keepdims=True))).astype(bf16)
    valid_row = jnp.broadcast_to((gx_ref[TOK + 8 : TOK + 9, :TOK].astype(f32) > 0.5).astype(f32), (TOK, TOK))
    valid = valid_row.T[:, 0:1]
    total = t_dot(dlog, misc_ref[0:16, :])
    for piece in pieces:
        total = total + piece[0:TOK, :].astype(f32)
    resid = resid_ref[...]
    rinv = lax.rsqrt(jnp.mean(resid * resid, axis=1, keepdims=True) + EPS)
    u = total * misc_ref[17:18, :].astype(f32)
    g = gx_ref[0:TOK, :].astype(f32) * valid
    dresid = g + rinv * u - resid * (rinv * rinv * rinv) * jnp.mean(u * resid, axis=1, keepdims=True)
    dresid_ref[...] = dresid
    dattn_ref[...] = dresid.astype(bf16)
    small_ref[0:16, :] = dot(dlog, n2_ref[...])
    gain = jnp.sum(total * resid * rinv, axis=0, keepdims=True)
    line = lax.broadcasted_iota(jnp.int32, (16, D), 0)
    small_ref[16:32, :] = jnp.where(line == 1, gain, 0.0)


def kernel_back_o(where, da_own, da_sib, mixed_ref, *rest):
    pieces = rest[:16]
    dmixed_ref = rest[16]
    grads = rest[17:33]
    w, wg, sems, gsems = rest[33:]
    z, x = where[0], where[2]
    copies = o_copies(pieces, w, sems, z, x)
    for item in copies:
        item.start()
    dattn = jnp.concatenate([da_own[...], da_sib[...]], axis=0)
    wg[...] = t_dot(mixed_ref[...], dattn).astype(bf16)
    for item in copies:
        item.wait()
    outs = []
    for j in range(4):
        for k in range(4):
            start = pl.multiple_of(((z ^ j) * 4 + (x ^ k)) * 48, 16)
            outs.append(
                pltpu.make_async_copy(wg.at[pl.ds(start, 48), :], grads[j * 4 + k], gsems.at[j * 4 + k])
            )
    for item in outs:
        item.start()
    dmixed_ref[...] = dot_t(dattn, w[...]).astype(bf16)
    for item in outs:
        item.wait()


def kernel_back(where, xo, xs, dmixed_ref, normed_ref, q_ref, k_ref, v_ref, small_ref, cos_ref, sin_ref, *rest):
    pieces = rest[:16]
    own_ref, sib_ref = rest[16:18]
    grads = rest[18:34]
    w, dq_s, dk_s, dv_s, dcat, wg, sems, gsems = rest[34:]
    z, x = where[0], where[2]
    copies = piece_copies(pieces, w, sems, z, x)
    for item in copies:
        item.start()
    for part, src in enumerate((xo, xs)):
        ok = allowed_mask(src[TOK:EXT, :TOK].astype(f32))
        ok3 = jnp.concatenate([ok.astype(f32)] * 3, axis=0) > 0.5
        rows = slice(part * TOK, (part + 1) * TOK)
        for a in range(4):
            keys = k_ref[rows, a * 64 : (a + 1) * 64]
            vals = v_ref[rows, a * 64 : (a + 1) * 64]
            heads = [slice((3 * a + g) * 64, (3 * a + g + 1) * 64) for g in range(3)]
            q3 = jnp.concatenate([q_ref[rows, hd] for hd in heads], axis=0)
            dm3 = jnp.concatenate([dmixed_ref[rows, hd] for hd in heads], axis=0)
            scores = jnp.where(ok3, dot_t(q3, keys) * 0.125, NEG)
            top = jnp.max(scores, axis=1, keepdims=True)
            expo = jnp.exp(scores - top)
            probs = expo / jnp.sum(expo, axis=1, keepdims=True)
            dprobs = dot_t(dm3, vals)
            dv_s[rows, a * 64 : (a + 1) * 64] = t_dot(probs.astype(bf16), dm3)
            ds = (probs * (dprobs - jnp.sum(probs * dprobs, axis=1, keepdims=True))).astype(bf16)
            dq3 = dot(ds, keys) * 0.125
            for g in range(3):
                dq_s[rows, heads[g]] = dq3[g * TOK : (g + 1) * TOK, :]
            dk_s[rows, a * 64 : (a + 1) * 64] = t_dot(ds, q3) * 0.125
    cos_full, sin_full = cos_ref[...], -sin_ref[...]
    dcat[:, 0:HQ] = turn(dq_s[...], cos_full, sin_full).astype(bf16)
    dcat[:, HQ : HQ + HK] = turn(dk_s[...], cos_full, sin_full).astype(bf16)
    dcat[:, HQ + HK : QKV] = dv_s[...].astype(bf16)
    for item in copies:
        item.wait()
    misc_gain = dot_t(
        (
            lax.broadcasted_iota(jnp.int32, (128, 128), 0)
            == lax.broadcasted_iota(jnp.int32, (128, 128), 1)
        ).astype(f32).astype(bf16),
        w[:, QKV:],
    )[16:17, :]
    del misc_gain
    dnormed = dot_t(dcat[...], w[:, 0:QKV])
    own_ref[...] = dnormed[:TOK, :]
    sib_ref[...] = dnormed[TOK:, :]
    xin = jnp.concatenate([xo[:TOK, :], xs[:TOK, :]], axis=0).astype(f32)
    rinv = lax.rsqrt(jnp.mean(xin * xin, axis=1, keepdims=True) + EPS)
    gain = jnp.sum(dnormed * xin * rinv, axis=0, keepdims=True)
    line = lax.broadcasted_iota(jnp.int32, (32, D), 0)
    small = small_ref[...] + jnp.where(line == 16, gain, 0.0)
    small = jnp.concatenate([small, jnp.zeros((96, D), f32)], axis=0).astype(bf16)
    eye = (
        lax.broadcasted_iota(jnp.int32, (128, 128), 0) == lax.broadcasted_iota(jnp.int32, (128, 128), 1)
    ).astype(f32).astype(bf16)
    wg[:, 0:QKV] = t_dot(normed_ref[...], dcat[...]).astype(bf16)
    wg[:, QKV:] = t_dot(small, eye).astype(bf16)
    outs = []
    for j in range(4):
        for k in range(4):
            for b in range(2):
                start = pl.multiple_of((((z ^ j) * 2 + b) * 4 + (x ^ k)) * 48, 16)
                outs.append(
                    pltpu.make_async_copy(
                        wg.at[pl.ds(start, 48), :],
                        grads[j * 4 + k].at[pl.ds(48 * b, 48), :],
                        gsems.at[(j * 4 + k) * 2 + b],
                    )
                )
    for item in outs:
        item.start()
    for item in outs:
        item.wait()


def kernel_token_grad(xo, dresid_ref, own_ref, recv_ref, misc_ref, out_ref):
    xin = xo[:TOK, :].astype(f32)
    rinv = lax.rsqrt(jnp.mean(xin * xin, axis=1, keepdims=True) + EPS)
    u = (own_ref[...] + recv_ref[...]) * misc_ref[16:17, :].astype(f32)
    out = dresid_ref[...] + rinv * u - xin * (rinv * rinv * rinv) * jnp.mean(u * xin, axis=1, keepdims=True)
    out_ref[...] = out.astype(bf16)


def kernel_block_out(gx_ref, resid_ref, *rest):
    pieces, out_ref = rest[:8], rest[8]
    valid_row = jnp.broadcast_to((gx_ref[TOK + 8 : TOK + 9, :TOK].astype(f32) > 0.5).astype(f32), (TOK, TOK))
    valid = valid_row.T[:, 0:1]
    total = resid_ref[...]
    for piece in pieces:
        total = total + piece[...].astype(f32)
    out_ref[...] = (total * valid).astype(bf16)


def call(body, outs, ins, scratch=(), mib=60, flops=0, nbytes=0, name=None):
    return pl.pallas_call(
        body,
        out_shape=[jax.ShapeDtypeStruct(shape, dtype) for shape, dtype, _ in outs],
        in_specs=[spec for _, spec in ins],
        out_specs=[spec for _, _, spec in outs],
        scratch_shapes=list(scratch),
        compiler_params=params(mib),
        cost_estimate=pl.CostEstimate(flops=flops, bytes_accessed=nbytes, transcendentals=0),
        name=name,
    )(*[value for value, _ in ins])


def sum_pieces(pieces):
    total = pieces[0].astype(f32)
    for piece in pieces[1:]:
        total = total + piece.astype(f32)
    return total


def on_device(
    tokens, segment_ids, routes, cotangent, attn_gain, query_weight, key_weight, value_weight,
    output_weight, expert_gain, router_weight, expert_in, expert_out,
):
    V, A, S = spec_vmem(), spec_any(), spec_smem()
    iz, ih, ix, ic, il = [lax.axis_index(name) for name in AX]
    where = jnp.stack([iz, ih, ix, ic, il]).astype(jnp.int32)
    cos_np, sin_np = rope_tables()
    cos_full, sin_full = jnp.asarray(cos_np), jnp.asarray(sin_np)

    ints = jnp.concatenate(
        [routes.reshape(TOK, TOPK).T, segment_ids.reshape(1, TOK), jnp.zeros((7, TOK), jnp.int32)], axis=0
    ).astype(bf16)
    ints = jnp.pad(ints, ((0, 0), (0, D - TOK)))
    x_own = jnp.concatenate([tokens.reshape(TOK, D), ints], axis=0)
    g_own = jnp.concatenate([cotangent.reshape(TOK, D), ints], axis=0)
    x_sib = send(x_own, dc=1)

    small = jnp.concatenate(
        [router_weight, attn_gain[:, None], expert_gain[:, None], jnp.zeros((12, 110), bf16)], axis=1
    )
    q4 = query_weight.reshape(12, 4, 2, 192)
    k4 = key_weight.reshape(12, 4, 2, 64)
    v4 = value_weight.reshape(12, 4, 2, 64)
    for_core = [
        jnp.concatenate(
            [
                q4[:, :, core].reshape(12, HQ),
                k4[:, :, core].reshape(12, HK),
                v4[:, :, core].reshape(12, HK),
                small,
                output_weight,
            ],
            axis=1,
        )
        for core in range(2)
    ]
    packed = jnp.stack([for_core[0], for_core[0], for_core[1], for_core[1]])
    packed = lax.all_to_all(packed, ("c", "yl"), split_axis=0, concat_axis=0, tiled=True)
    qkv48 = packed[:, :, :QKVM].reshape(48, QKVM)
    o48 = packed[:, :, QKVM:].reshape(48, D)
    qkv_other = send(qkv48, dh=1)
    o_other = send(o48, dh=1)
    qkv96 = jnp.where(
        ih == 0,
        jnp.concatenate([qkv48, qkv_other], axis=0),
        jnp.concatenate([qkv_other, qkv48], axis=0),
    )
    o_mine = jnp.where(ih == ic, o48, o_other)
    pairs = [(j, k) for j in range(4) for k in range(4)]
    qkv_pieces = [qkv96 if (j, k) == (0, 0) else send(qkv96, dz=j, dx=k) for j, k in pairs]
    o_pieces = [o_mine if (j, k) == (0, 0) else send(o_mine, dz=j, dx=k) for j, k in pairs]

    e_in = lax.all_to_all(expert_in, ("x", "c"), split_axis=0, concat_axis=0, tiled=True).reshape(192, 1024)
    e_out = lax.all_to_all(expert_out, ("x", "c"), split_axis=0, concat_axis=0, tiled=True).reshape(64, D)
    e_pack = jnp.concatenate(
        [e_in, jnp.concatenate([e_out[:, t * 512 : (t + 1) * 512] for t in range(3)], axis=0)], axis=1
    )
    e_pairs = [(j, b) for j in range(4) for b in range(2)]
    e_pieces = [e_pack if (j, b) == (0, 0) else send(e_pack, dz=j, dh=b) for j, b in e_pairs]

    p_pairs = [(k, b) for k in range(4) for b in range(2)]

    def spread(value):
        mine = [value if (k, b) == (0, 0) else send(value, dx=k, dl=b) for k, b in p_pairs]
        return mine + [send(item, dc=1) for item in mine]

    gx_pieces = spread(g_own)

    normed, q_b, k_b, v_b, mixed, misc = call(
        kernel_attn,
        [
            ((256, D), bf16, V), ((256, HQ), bf16, V), ((256, HK), bf16, V), ((256, HK), bf16, V),
            ((256, HQ), bf16, V), ((128, D), bf16, V),
        ],
        [(where, S), (x_own, V), (x_sib, V), (cos_full, V), (sin_full, V)] + [(p, A) for p in qkv_pieces],
        [pltpu.VMEM((D, QKVM), bf16), pltpu.SemaphoreType.DMA((32,))],
        flops=2 * 256 * D * QKV, nbytes=8 * 2**20, name="attention",
    )
    part_own, part_sib = call(
        kernel_oproj,
        [((TOK, D), f32, V), ((TOK, D), f32, V)],
        [(where, S), (mixed, V)] + [(p, A) for p in o_pieces],
        [pltpu.VMEM((HQ, D), bf16), pltpu.SemaphoreType.DMA((16,))],
        flops=2 * 256 * D * HQ, nbytes=4 * 2**20, name="output_projection",
    )
    part_recv = send(part_sib, dc=1)
    resid, n2, gates = call(
        kernel_resid,
        [((TOK, D), f32, V), ((TOK, D), bf16, V), ((16, TOK), f32, V)],
        [(x_own, V), (part_own, V), (part_recv, V), (misc, V)],
        flops=10**7, nbytes=3 * 2**20, name="residual_norm",
    )
    n2_pieces = spread(n2)
    outs = call(
        kernel_expert,
        [((8, EXT, D), bf16, A), ((8, EXT, D), bf16, A), ((8, TOK, D), bf16, A), ((8, TOK, D), bf16, A)]
        + [((192, D), bf16, A)] * 8,
        [(where, S), (misc, V)] + [(p, A) for p in n2_pieces + gx_pieces + e_pieces],
        [
            pltpu.VMEM((2048, D), bf16), pltpu.VMEM((16, EXT, D), bf16),
            pltpu.VMEM((D, 1024), bf16), pltpu.VMEM((F, D), bf16),
            pltpu.VMEM((1024, D), bf16), pltpu.VMEM((1024, D), bf16),
            pltpu.VMEM((1024, F), bf16), pltpu.VMEM((1024, 1024), bf16),
            pltpu.VMEM((16, TOK), f32), pltpu.VMEM((16, TOK), f32), pltpu.VMEM((16, TOK), f32),
            pltpu.VMEM((4, EXT, D), bf16), pltpu.VMEM((4, TOK, D), bf16),
            pltpu.VMEM((D, D), bf16),
            pltpu.SemaphoreType.DMA((16,)), pltpu.SemaphoreType.DMA((16,)),
            pltpu.SemaphoreType.DMA((32,)), pltpu.SemaphoreType.DMA((2,)),
            pltpu.SemaphoreType.DMA((8,)),
        ],
        flops=18 * 10**9, nbytes=40 * 2**20, name="experts",
    )
    dn_own, dn_sib, mix_own, mix_sib = outs[:4]
    e_grads = outs[4:]

    def gather_sums(own, sib, rows):
        recv = send(sib, dc=1)
        sums = call(
            kernel_pair_sum, [((rows, D), bf16, V)] * 8, [(own, V), (recv, V)],
            flops=10**7, nbytes=10 * 2**20, name="pair_sum",
        )
        return [sums[i] if (k, b) == (0, 0) else send(sums[i], dx=k, dl=b) for i, (k, b) in enumerate(p_pairs)]

    dn_pieces = gather_sums(dn_own, dn_sib, EXT)
    dresid, dattn, small_grad = call(
        kernel_home,
        [((TOK, D), f32, V), ((TOK, D), bf16, V), ((32, D), f32, V)],
        [(where, S), (g_own, V), (resid, V), (n2, V), (gates, V), (misc, V)] + [(p, V) for p in dn_pieces],
        [pltpu.VMEM((16, TOK), f32)],
        flops=10**8, nbytes=6 * 2**20, name="home_gradient",
    )
    dattn_sib = send(dattn, dc=1)
    outs = call(
        kernel_back_o,
        [((256, HQ), bf16, V)] + [((48, D), bf16, A)] * 16,
        [(where, S), (dattn, V), (dattn_sib, V), (mixed, V)] + [(p, A) for p in o_pieces],
        [
            pltpu.VMEM((HQ, D), bf16), pltpu.VMEM((HQ, D), bf16),
            pltpu.SemaphoreType.DMA((16,)), pltpu.SemaphoreType.DMA((16,)),
        ],
        flops=4 * 256 * D * HQ, nbytes=6 * 2**20, name="output_back",
    )
    dmixed, o_grads = outs[0], outs[1:]
    outs = call(
        kernel_back,
        [((TOK, D), f32, V), ((TOK, D), f32, V)] + [((96, QKVM), bf16, A)] * 16,
        [
            (where, S), (x_own, V), (x_sib, V), (dmixed, V), (normed, V), (q_b, V), (k_b, V), (v_b, V),
            (small_grad, V), (cos_full, V), (sin_full, V),
        ]
        + [(p, A) for p in qkv_pieces],
        [
            pltpu.VMEM((D, QKVM), bf16), pltpu.VMEM((256, HQ), f32), pltpu.VMEM((256, HK), f32),
            pltpu.VMEM((256, HK), f32), pltpu.VMEM((256, QKV), bf16), pltpu.VMEM((D, QKVM), bf16),
            pltpu.SemaphoreType.DMA((32,)), pltpu.SemaphoreType.DMA((32,)),
        ],
        flops=4 * 256 * D * QKV, nbytes=12 * 2**20, name="attention_back",
    )
    dn1_own, dn1_sib, qkv_grads = outs[0], outs[1], outs[2:]
    dn1_recv = send(dn1_sib, dc=1)
    (token_grad,) = call(
        kernel_token_grad, [((TOK, D), bf16, V)],
        [(x_own, V), (dresid, V), (dn1_own, V), (dn1_recv, V), (misc, V)],
        flops=10**7, nbytes=3 * 2**20, name="token_gradient",
    )
    mix_pieces = gather_sums(mix_own, mix_sib, TOK)
    (block_out,) = call(
        kernel_block_out, [((TOK, D), bf16, V)], [(g_own, V), (resid, V)] + [(p, V) for p in mix_pieces],
        flops=10**7, nbytes=5 * 2**20, name="block_output",
    )

    e_sum = sum_pieces(
        [e_grads[0]] + [send(e_grads[i], dz=j, dh=b) for i, (j, b) in enumerate(e_pairs) if i]
    ).astype(bf16)
    ge_in = lax.all_to_all(e_sum[:, :1024].reshape(8, 24, 1024), ("x", "c"), split_axis=0, concat_axis=0, tiled=True)
    ge_out = jnp.concatenate([e_sum[t * 64 : (t + 1) * 64, 1024:] for t in range(3)], axis=1)
    ge_out = lax.all_to_all(ge_out.reshape(8, 8, D), ("x", "c"), split_axis=0, concat_axis=0, tiled=True)

    o_sum = sum_pieces([o_grads[0]] + [send(o_grads[i], dz=j, dx=k) for i, (j, k) in enumerate(pairs) if i])
    o_sum = o_sum.astype(bf16)
    o_swap = send(o_sum, dh=1)
    o_sum = o_sum.astype(f32) + o_swap.astype(f32)
    qkv_sum = sum_pieces([qkv_grads[0]] + [send(qkv_grads[i], dz=j, dx=k) for i, (j, k) in enumerate(pairs) if i])
    keep = jnp.where(ih == 0, qkv_sum[:48], qkv_sum[48:])
    give = jnp.where(ih == 0, qkv_sum[48:], qkv_sum[:48])
    qkv_sum = (keep + send(give.astype(bf16), dh=1).astype(f32)).astype(bf16)
    o_part = jnp.where(ih == ic, o_sum, 0.0).astype(bf16)
    back = jnp.concatenate([qkv_sum, o_part], axis=1).reshape(4, 12, QKVM + D)
    back = lax.all_to_all(back, ("c", "yl"), split_axis=0, concat_axis=0, tiled=True).astype(f32)
    back = back[0::2] + back[1::2]
    dq = jnp.stack([back[core, :, :HQ].reshape(12, 4, 192) for core in range(2)], axis=2).reshape(12, D)
    dk = jnp.stack([back[core, :, HQ : HQ + HK].reshape(12, 4, 64) for core in range(2)], axis=2).reshape(12, 512)
    dv = jnp.stack([back[core, :, HQ + HK : QKV].reshape(12, 4, 64) for core in range(2)], axis=2).reshape(12, 512)
    tail = back[0] + back[1]
    d_o = tail[:, QKVM:]
    d_small = tail[:, QKV:QKVM]
    return (
        block_out.reshape(2, SEQ, D),
        token_grad.reshape(2, SEQ, D),
        d_small[:, 16],
        dq,
        dk,
        dv,
        d_o,
        d_small[:, 17],
        d_small[:, :16],
        ge_in.astype(f32),
        ge_out.astype(f32),
    )


def solution(mesh):
    devices = mesh.devices.reshape(DIMS) if hasattr(mesh, "devices") else None
    fine = Mesh(devices, AX)
    every = ("z", "yh", "x", "c", "yl")
    dp = ("z", "yh", "x", "c")
    in_specs = (
        P(every, None, None), P(every, None), P(every, None, None), P(every, None, None), P(every),
        P(every, None), P(every, None), P(every, None), P(every, None), P(every), P(every, None),
        P("yl", dp, None), P("yl", dp, None),
    )
    out_specs = (
        P(every, None, None), P(every, None, None), P(every), P(every, None), P(every, None),
        P(every, None), P(every, None), P(every), P(every, None), P("yl", dp, None), P("yl", dp, None),
    )
    return jax.shard_map(on_device, mesh=fine, in_specs=in_specs, out_specs=out_specs, check_vma=False)
```

```python
import functools

import jax
import jax.numpy as jnp
import numpy as np
from jax import lax
from jax.experimental import pallas as pl
from jax.experimental.pallas import tpu as pltpu
from jax.sharding import Mesh
from jax.sharding import PartitionSpec as P

D = 1536
Q_HEADS = 24
KV_HEADS = 8
HEAD_DIM = 64
F = 512
TOPK = 8
EXPERTS = 16
SEQ = 64
CAP = 32

AX = ("z", "yh", "x", "c", "yl")
DIMS = (4, 2, 4, 2, 2)
EPS = 1e-5
NEG = -1e30
TOK = 128
EXT = 144
HQ = 192
QK = 256
QKV = 320
QKVM = 384
ROWS = 1024
bf16 = jnp.bfloat16
f32 = jnp.float32


def coords_list():
    return list(np.ndindex(*DIMS))


def send(value, dz=0, dh=0, dx=0, dc=0, dl=0):
    flat = {pos: i for i, pos in enumerate(coords_list())}
    pairs = [
        (i, flat[(z ^ dz, h ^ dh, x ^ dx, c ^ dc, l ^ dl)])
        for (z, h, x, c, l), i in flat.items()
    ]
    return lax.ppermute(value, AX, pairs)


def dot(a, b):
    return jnp.dot(a, b, preferred_element_type=f32)


def dot_t(a, b):
    return lax.dot_general(a, b, (((1,), (1,)), ((), ())), preferred_element_type=f32)


def t_dot(a, b):
    return lax.dot_general(a, b, (((0,), (0,)), ((), ())), preferred_element_type=f32)


def params(mib=60):
    return pltpu.CompilerParams(vmem_limit_bytes=mib * 2**20)


def rope_tables():
    angle = np.arange(SEQ)[:, None] * (10000.0 ** (-np.arange(32) * 2.0 / 64))[None, :]
    cosine, sine = np.cos(angle), np.sin(angle)
    cos_full = np.concatenate([cosine, cosine] * 2, axis=1)
    sin_full = np.concatenate([-sine, sine] * 2, axis=1)
    return np.tile(cos_full, (4, 1)).astype(np.float32), np.tile(sin_full, (4, 1)).astype(np.float32)


def turn(values, cos_full, sin_full):
    width = values.shape[1]
    lane = lax.broadcasted_iota(jnp.int32, values.shape, 1)
    ahead = pltpu.roll(values, width - 32, 1)
    behind = pltpu.roll(values, 32, 1)
    partner = jnp.where((lane % 64) < 32, ahead, behind)
    copies = width // 128
    cos_wide = jnp.concatenate([cos_full] * copies, axis=1)
    sin_wide = jnp.concatenate([sin_full] * copies, axis=1)
    return values * cos_wide + partner * sin_wide


def allowed_mask(ints):
    row = jnp.broadcast_to(ints[8:9, :], (TOK, TOK))
    col = row.T
    p = lax.broadcasted_iota(jnp.int32, (TOK, TOK), 0)
    t = lax.broadcasted_iota(jnp.int32, (TOK, TOK), 1)
    return (row == col) & (t <= p) & ((p < SEQ) == (t < SEQ))


def qkv_copies(pieces, target, sems, h, x):
    copies = []
    for k in range(4):
        for b in range(2):
            for zz in range(4):
                start = pl.multiple_of(((zz * 2 + (h ^ b)) * 4 + (x ^ k)) * 48, 16)
                copies.append(
                    pltpu.make_async_copy(
                        pieces[k].at[b, zz], target.at[pl.ds(start, 48), :], sems.at[(k * 2 + b) * 4 + zz]
                    )
                )
    return copies


def o_copies(pieces, target, sems, x):
    return [
        pltpu.make_async_copy(
            pieces[k], target.at[pl.ds(pl.multiple_of((x ^ k) * 48, 16), 48), :], sems.at[k]
        )
        for k in range(4)
    ]


def spec_any():
    return pl.BlockSpec(memory_space=pl.ANY)


def spec_vmem():
    return pl.BlockSpec(memory_space=pltpu.VMEM)


def spec_smem():
    return pl.BlockSpec(memory_space=pltpu.SMEM)


def unit(size):
    row = lax.broadcasted_iota(jnp.int32, (size, size), 0)
    return (row == lax.broadcasted_iota(jnp.int32, (size, size), 1)).astype(f32).astype(bf16)


def kernel_attn(where, cos_ref, sin_ref, *rest):
    x_in, w_in, wo_in = rest[:8], rest[8:12], rest[12:16]
    normed_ref, qk_ref, v_ref, mixed_ref, misc_ref, own_ref, sib_ref = rest[16:23]
    w, wo, sems, osems = rest[23:]
    copies = qkv_copies(w_in, w, sems, where[1], where[2])
    more = o_copies(wo_in, wo, osems, where[2])
    for item in copies + more:
        item.start()
    for item in copies:
        item.wait()
    misc = dot_t(unit(64), w[:, QKV:])
    misc_ref[...] = misc.astype(bf16)
    gain = misc[16:17, :]
    for m in range(8):
        rows = slice(m * TOK, (m + 1) * TOK)
        xin = x_in[m][0:TOK, :].astype(f32)
        rinv = lax.rsqrt(jnp.mean(xin * xin, axis=1, keepdims=True) + EPS)
        normed_ref[rows, :] = (xin * rinv * gain).astype(bf16)
    cos_full, sin_full = cos_ref[...], sin_ref[...]
    for m in range(4):
        rows = slice(m * 256, (m + 1) * 256)
        qkv = dot(normed_ref[rows, :], w[:, 0:QKVM])
        qk_ref[rows, :] = turn(qkv[:, 0:QK], cos_full, sin_full).astype(bf16)
        v_ref[rows, :] = qkv[:, QK:QKVM].astype(bf16)
    for m in range(8):
        ok = allowed_mask(x_in[m][TOK:EXT, :TOK].astype(f32))
        ok3 = jnp.concatenate([ok.astype(f32)] * 3, axis=0) > 0.5
        rows = slice(m * TOK, (m + 1) * TOK)
        keys = qk_ref[rows, HQ:QK]
        vals = v_ref[rows, 0:64]
        q3 = jnp.concatenate([qk_ref[rows, g * 64 : (g + 1) * 64] for g in range(3)], axis=0)
        scores = jnp.where(ok3, dot_t(q3, keys) * 0.125, NEG)
        top = jnp.max(scores, axis=1, keepdims=True)
        expo = jnp.exp(scores - top)
        probs = (expo / jnp.sum(expo, axis=1, keepdims=True)).astype(bf16)
        out = dot(probs, vals).astype(bf16)
        for g in range(3):
            mixed_ref[rows, g * 64 : (g + 1) * 64] = out[g * TOK : (g + 1) * TOK, :]
    for item in more:
        item.wait()
    for m in range(4):
        rows = slice(m * TOK, (m + 1) * TOK)
        own_ref[m] = dot(mixed_ref[rows, :], wo[...])
        rows = slice((4 + m) * TOK, (5 + m) * TOK)
        sib_ref[m] = dot(mixed_ref[rows, :], wo[...]).astype(bf16)


def kernel_core_sum(own_ref, recv_ref, *outs):
    for m in range(4):
        outs[m][...] = (own_ref[m] + recv_ref[m].astype(f32)).astype(bf16)


def chosen_gates(misc, n2, ints):
    logits = dot_t(misc, n2)
    expert = lax.broadcasted_iota(jnp.int32, logits.shape, 0).astype(f32)
    hot = jnp.zeros(logits.shape, f32)
    for k in range(TOPK):
        hot = jnp.maximum(hot, (expert == ints[k : k + 1, :]).astype(f32))
    masked = jnp.where(hot > 0.5, logits, NEG)
    expo = jnp.where(hot > 0.5, jnp.exp(masked - jnp.max(masked, axis=0, keepdims=True)), 0.0)
    return expo / jnp.sum(expo, axis=0, keepdims=True)


def kernel_resid(xo, p0, p1, p2, p3, misc_ref, resid_ref, n2_ref, gates_ref, na_ref, nb_ref):
    resid = xo[:TOK, :].astype(f32)
    for piece in (p0, p1, p2, p3):
        resid = resid + piece[...].astype(f32)
    resid_ref[...] = resid
    rinv = lax.rsqrt(jnp.mean(resid * resid, axis=1, keepdims=True) + EPS)
    n2 = (resid * rinv * misc_ref[17:18, :].astype(f32)).astype(bf16)
    n2_ref[...] = n2
    for m in range(8):
        na_ref[m] = n2[:SEQ, :]
        nb_ref[m] = n2[SEQ:, :]
    gates_ref[...] = chosen_gates(misc_ref[0:16, :], n2, xo[TOK:EXT, :TOK].astype(f32))


def kernel_expert(half, where, misc_ref, n2_own, n2_sib, w_ref, *rest):
    gx_in = rest[:4]
    dn_own, mix_own, disp, dslot, hid, dgu = rest[4:10]
    dn_sib, mix_sib = rest[10:14], rest[14:18]
    n2, gx, win, wout, slot_s, gate_s, ints_s, n2_sem, gx_sem, w_sem = rest[18:]
    x, c, l = where[2], where[3], where[4]
    me = (l * 8 + x * 2 + c).astype(f32)
    w_copies = []
    for blk in range(8):
        w_copies.append(
            pltpu.make_async_copy(
                w_ref.at[pl.ds(blk * 192, 192), pl.ds(0, 1024)], win.at[pl.ds(blk * 192, 192), :], w_sem.at[blk * 4]
            )
        )
        for t in range(3):
            w_copies.append(
                pltpu.make_async_copy(
                    w_ref.at[pl.ds(blk * 192 + 64 * t, 64), pl.ds(1024, 512)],
                    wout.at[pl.ds(blk * 64, 64), pl.ds(512 * t, 512)],
                    w_sem.at[blk * 4 + 1 + t],
                )
            )
    n2_copies = [
        pltpu.make_async_copy(n2_own, n2.at[pl.ds(0, 8)], n2_sem.at[0]),
        pltpu.make_async_copy(n2_sib, n2.at[pl.ds(8, 8)], n2_sem.at[1]),
    ]
    gx_copies = []
    for core in range(2):
        for k in range(4):
            for b in range(2):
                at = core * 8 + (x ^ k) * 2 + (l ^ b)
                g_src = gx_in[core * 2 + b].at[k]
                gx_copies.append(
                    pltpu.make_async_copy(
                        g_src.at[pl.ds(SEQ * half, SEQ), :], gx.at[at, pl.ds(0, SEQ), :], gx_sem.at[(core * 8 + k * 2 + b) * 2]
                    )
                )
                gx_copies.append(
                    pltpu.make_async_copy(
                        g_src.at[pl.ds(TOK, 16), :], gx.at[at, pl.ds(SEQ, 16), :], gx_sem.at[(core * 8 + k * 2 + b) * 2 + 1]
                    )
                )
    for item in gx_copies + n2_copies + w_copies:
        item.start()
    for item in gx_copies + n2_copies:
        item.wait()
    for m in range(16):
        ints_s[:, SEQ * m : SEQ * (m + 1)] = gx[m, SEQ : SEQ + 16, SEQ * half : SEQ * (half + 1)].astype(f32)
    token = lax.broadcasted_iota(jnp.int32, (TOK, TOK), 0)
    after = lax.broadcasted_iota(jnp.int32, (TOK, TOK), 1)
    before = ((token < after) & ((token < SEQ) == (after < SEQ))).astype(f32).astype(bf16)
    for core in range(2):
        lanes = slice(core * 512, core * 512 + 512)
        ints = ints_s[:, lanes]
        gates = chosen_gates(misc_ref[0:16, :], n2[8 * core : 8 * core + 8].reshape(512, D), ints)
        expert = lax.broadcasted_iota(jnp.int32, gates.shape, 0).astype(f32)
        gate = jnp.sum(jnp.where(expert == me, gates, 0.0), axis=0, keepdims=True)
        hit = jnp.max((ints[0:8, :] == me).astype(f32), axis=0, keepdims=True)
        hit = hit * (ints[8:9, :] > 0.5).astype(f32)
        rank = jnp.concatenate(
            [
                dot(jnp.broadcast_to(hit[:, u * TOK : (u + 1) * TOK], (16, TOK)).astype(bf16), before)[0:1, :]
                for u in range(4)
            ],
            axis=1,
        )
        slot = jnp.where((hit > 0.5) & (rank < CAP - 0.5), rank, -1.0)
        for q in range(8):
            slot_s[core * 8 + q : core * 8 + q + 1, :] = slot[:, q * SEQ : (q + 1) * SEQ]
            gate_s[core * 8 + q : core * 8 + q + 1, :] = gate[:, q * SEQ : (q + 1) * SEQ]
    for item in w_copies:
        item.wait()

    def one_chunk(i, carry):
        rows = pl.ds(pl.multiple_of(i * 256, 256), 256)
        slot_iota = lax.broadcasted_iota(jnp.int32, (CAP, SEQ), 0).astype(f32)
        hots, gate_cols, g_parts = [], [], []
        for q in range(8):
            m = i * 8 + q
            hot = (slot_iota == slot_s[pl.ds(m, 1), :]).astype(f32)
            gate_col = jnp.sum(hot * gate_s[pl.ds(m, 1), :], axis=1, keepdims=True)
            hot_b = hot.astype(bf16)
            hots.append(hot_b)
            gate_cols.append(gate_col)
            srows = pl.ds(pl.multiple_of(i * 256 + q * CAP, CAP), CAP)
            disp[srows, :] = dot(hot_b, n2[m]).astype(bf16)
            gsl = dot(hot_b, gx[m, 0:SEQ, :])
            g_parts.append(gsl)
            dslot[srows, :] = (gate_col * gsl).astype(bf16)
        gup = dot(disp[rows, :], win[...])
        gate_part, up_part = gup[:, :F], gup[:, F:]
        sig = jax.nn.sigmoid(gate_part)
        hidden = (gate_part * sig * up_part).astype(bf16)
        hid[rows, :] = hidden
        out_rows = dot(hidden, wout[...]).astype(bf16).astype(f32)
        dhid = dot_t(dslot[rows, :], wout[...])
        silu_grad = sig * (1.0 + gate_part * (1.0 - sig))
        dg = jnp.concatenate([dhid * up_part * silu_grad, dhid * gate_part * sig], axis=1).astype(bf16)
        dgu[rows, :] = dg
        din = dot_t(dg, win[...]).astype(bf16)

        def give(dn_refs, mix_refs):
            for q in range(8):
                dn_ref, mix_ref = dn_refs[q], mix_refs[q]
                part = slice(q * CAP, (q + 1) * CAP)
                dgate = jnp.sum(g_parts[q] * out_rows[part, :], axis=1, keepdims=True)
                dgate_row = jnp.sum(hots[q].astype(f32) * dgate, axis=0, keepdims=True)
                high = dgate_row.astype(bf16).astype(f32)
                low = dgate_row - high
                line = lax.broadcasted_iota(jnp.int32, (16, SEQ), 0)
                extra = jnp.where(line == 2 * c, high, 0.0) + jnp.where(line == 2 * c + 1, low, 0.0)
                dn_ref[0:SEQ, :] = t_dot(hots[q], din[part, :]).astype(bf16)
                dn_ref[SEQ : SEQ + 16, :] = jnp.zeros((16, D), bf16)
                dn_ref[SEQ : SEQ + 16, 0:SEQ] = extra.astype(bf16)
                weighted = (gate_cols[q] * out_rows[part, :]).astype(bf16)
                mix_ref[...] = t_dot(hots[q], weighted).astype(bf16)

        @pl.when(i == 0)
        def _():
            give([dn_own.at[q] for q in range(8)], [mix_own.at[q] for q in range(8)])

        @pl.when(i == 1)
        def _():
            give([dn_sib[q // 2].at[q % 2] for q in range(8)], [mix_sib[q // 2].at[q % 2] for q in range(8)])

        return carry

    lax.fori_loop(0, 2, one_chunk, 0)


def kernel_expert_grads(disp_a, dslot_a, hid_a, dgu_a, disp_b, dslot_b, hid_b, dgu_b, wg):
    for n in range(6):
        cols = slice(n * 256, (n + 1) * 256)
        wg[cols, 0:1024] = (t_dot(disp_a[:, cols], dgu_a[...]) + t_dot(disp_b[:, cols], dgu_b[...])).astype(bf16)
    for n in range(2):
        cols = slice(n * 256, (n + 1) * 256)
        out_g = (t_dot(hid_a[:, cols], dslot_a[...]) + t_dot(hid_b[:, cols], dslot_b[...])).astype(bf16)
        for b in range(4):
            blk = n * 4 + b
            for t in range(3):
                wg[blk * 192 + t * 64 : blk * 192 + (t + 1) * 64, 1024:1536] = out_g[
                    b * 64 : (b + 1) * 64, t * 512 : (t + 1) * 512
                ]


def kernel_pair_sum(*refs):
    out = refs[-1]
    lines = 0
    for i in range(0, len(refs) - 1, 5):
        size = refs[i].shape[1]
        for m in range(8):
            total = refs[i][m].astype(f32) + refs[i + 1 + m // 2][m % 2].astype(f32)
            out[m, lines : lines + size, :] = total.astype(bf16)
        lines += size


def kernel_mix_sum(where, *refs):
    l = where[4]
    for out, line in ((refs[10], l), (refs[11], 1 - l)):
        for xx in range(4):
            for half in range(2):
                own, sib = refs[5 * half], refs[5 * half + 1 + xx]
                total = own[xx * 2 + line].astype(f32) + sib[line].astype(f32)
                out[xx, SEQ * half : SEQ * (half + 1), :] = total.astype(bf16)


def kernel_mix_pair(where, keep_ref, recv_ref, *outs):
    for k in range(4):
        xx = where[2] ^ k
        outs[k][...] = (keep_ref[xx].astype(f32) + recv_ref[xx].astype(f32)).astype(bf16)


def kernel_home(gx_ref, resid_ref, n2_ref, gates_ref, misc_ref, dn_a, dn_b, dresid_ref, dattn_ref, small_ref, dg_s):
    for xx in range(4):
        for ll in range(2):
            for half, dn in enumerate((dn_a, dn_b)):
                extra = dn[xx * 2 + ll, SEQ : SEQ + 16, 0:SEQ].astype(f32)
                first = ll * 8 + xx * 2
                lanes = slice(SEQ * half, SEQ * (half + 1))
                dg_s[first : first + 1, lanes] = extra[0:1, :] + extra[1:2, :]
                dg_s[first + 1 : first + 2, lanes] = extra[2:3, :] + extra[3:4, :]
    gates = gates_ref[...]
    dgates = dg_s[...]
    dlog = (gates * (dgates - jnp.sum(gates * dgates, axis=0, keepdims=True))).astype(bf16)
    valid_row = jnp.broadcast_to((gx_ref[TOK + 8 : TOK + 9, :TOK].astype(f32) > 0.5).astype(f32), (TOK, TOK))
    valid = valid_row.T[:, 0:1]
    total = t_dot(dlog, misc_ref[0:16, :])
    sums = []
    for dn in (dn_a, dn_b):
        part = dn[0, 0:SEQ, :].astype(f32)
        for m in range(1, 8):
            part = part + dn[m, 0:SEQ, :].astype(f32)
        sums.append(part)
    total = total + jnp.concatenate(sums, axis=0)
    resid = resid_ref[...]
    rinv = lax.rsqrt(jnp.mean(resid * resid, axis=1, keepdims=True) + EPS)
    u = total * misc_ref[17:18, :].astype(f32)
    g = gx_ref[0:TOK, :].astype(f32) * valid
    dresid = g + rinv * u - resid * (rinv * rinv * rinv) * jnp.mean(u * resid, axis=1, keepdims=True)
    dresid_ref[...] = dresid
    dattn_ref[...] = dresid.astype(bf16)
    small_ref[0:16, :] = dot(dlog, n2_ref[...])
    gain = jnp.sum(total * resid * rinv, axis=0, keepdims=True)
    line = lax.broadcasted_iota(jnp.int32, (16, D), 0)
    small_ref[16:32, :] = jnp.where(line == 1, gain, 0.0)


def kernel_back(where, normed_ref, qk_ref, v_ref, mixed_ref, small_ref, cos_ref, sin_ref, *rest):
    x_in, da_in, w_in, wo_in = rest[:8], rest[8:16], rest[16:20], rest[20:24]
    own_ref, sib_ref = rest[24:26]
    w_out, o_out = rest[26:30], rest[30:34]
    w, wo, da, dmixed, dqk, dcat, wg, og, sems, osems, gsems = rest[34:]
    h, x = where[1], where[2]
    o_in = o_copies(wo_in, wo, osems, x)
    copies = qkv_copies(w_in, w, sems, h, x)
    for item in o_in + copies:
        item.start()
    for m in range(8):
        da[m * TOK : (m + 1) * TOK, :] = da_in[m][...]
    for item in o_in:
        item.wait()
    for m in range(4):
        rows = slice(m * 256, (m + 1) * 256)
        dmixed[rows, :] = dot_t(da[rows, :], wo[...]).astype(bf16)
    for m in range(8):
        ok = allowed_mask(x_in[m][TOK:EXT, :TOK].astype(f32))
        ok3 = jnp.concatenate([ok.astype(f32)] * 3, axis=0) > 0.5
        rows = slice(m * TOK, (m + 1) * TOK)
        keys = qk_ref[rows, HQ:QK]
        vals = v_ref[rows, 0:64]
        q3 = jnp.concatenate([qk_ref[rows, g * 64 : (g + 1) * 64] for g in range(3)], axis=0)
        dm3 = jnp.concatenate([dmixed[rows, g * 64 : (g + 1) * 64] for g in range(3)], axis=0)
        scores = jnp.where(ok3, dot_t(q3, keys) * 0.125, NEG)
        top = jnp.max(scores, axis=1, keepdims=True)
        expo = jnp.exp(scores - top)
        probs = expo / jnp.sum(expo, axis=1, keepdims=True)
        dprobs = dot_t(dm3, vals)
        dcat[rows, QK:QKV] = t_dot(probs.astype(bf16), dm3).astype(bf16)
        ds = (probs * (dprobs - jnp.sum(probs * dprobs, axis=1, keepdims=True))).astype(bf16)
        dq3 = dot(ds, keys) * 0.125
        for g in range(3):
            dqk[rows, g * 64 : (g + 1) * 64] = dq3[g * TOK : (g + 1) * TOK, :]
        dqk[rows, HQ:QK] = t_dot(ds, q3) * 0.125
    cos_full, sin_full = cos_ref[...], -sin_ref[...]
    for m in range(4):
        rows = slice(m * 256, (m + 1) * 256)
        dcat[rows, 0:QK] = turn(dqk[rows, :], cos_full, sin_full).astype(bf16)
    dcat[:, QKV:] = jnp.zeros((ROWS, QKVM - QKV), bf16)
    for item in copies:
        item.wait()
    w[:, QKV:] = jnp.zeros((D, QKVM - QKV), bf16)
    gain = jnp.zeros((1, D), f32)
    for m in range(8):
        rows = slice(m * TOK, (m + 1) * TOK)
        dnormed = dot_t(dcat[rows, :], w[...])
        xin = x_in[m][0:TOK, :].astype(f32)
        rinv = lax.rsqrt(jnp.mean(xin * xin, axis=1, keepdims=True) + EPS)
        gain = gain + jnp.sum(dnormed * xin * rinv, axis=0, keepdims=True)
        if m < 4:
            own_ref[m] = dnormed
        else:
            sib_ref[m - 4] = dnormed.astype(bf16)
    line = lax.broadcasted_iota(jnp.int32, (32, D), 0)
    small = small_ref[...] + jnp.where(line == 16, gain, 0.0)
    small = jnp.concatenate([small, jnp.zeros((32, D), f32)], axis=0).astype(bf16)
    og[...] = t_dot(mixed_ref[...], da[...]).astype(bf16)
    wg[:, 0:QKVM] = t_dot(normed_ref[...], dcat[...]).astype(bf16)
    wg[:, QKV:] = t_dot(small, unit(64)).astype(bf16)
    outs = []
    for k in range(4):
        for b in range(2):
            for zz in range(4):
                start = pl.multiple_of(((zz * 2 + (h ^ b)) * 4 + (x ^ k)) * 48, 16)
                outs.append(
                    pltpu.make_async_copy(
                        wg.at[pl.ds(start, 48), :], w_out[k].at[b, zz], gsems.at[(k * 2 + b) * 4 + zz]
                    )
                )
        start = pl.multiple_of((x ^ k) * 48, 16)
        outs.append(pltpu.make_async_copy(og.at[pl.ds(start, 48), :], o_out[k], gsems.at[32 + k]))
    for item in outs:
        item.start()
    for item in outs:
        item.wait()


def kernel_dense_sum(where, *refs):
    w_in, o_in = refs[:4], refs[4:8]
    w_keep, w_give, o_keep, o_give = refs[8:]
    for b, out in enumerate((w_keep, w_give)):
        for zz in range(4):
            total = w_in[0][b, zz].astype(f32)
            for k in range(1, 4):
                total = total + w_in[k][b, zz].astype(f32)
            out[zz] = total.astype(bf16)
    total = o_in[0][...].astype(f32)
    for k in range(1, 4):
        total = total + o_in[k][...].astype(f32)
    here = where[1] == where[3]
    o_keep[...] = jnp.where(here, total, 0.0).astype(bf16)
    o_give[...] = jnp.where(here, 0.0, total).astype(bf16)


def kernel_token_grad(xo, dresid_ref, p0, p1, p2, p3, misc_ref, out_ref):
    xin = xo[:TOK, :].astype(f32)
    rinv = lax.rsqrt(jnp.mean(xin * xin, axis=1, keepdims=True) + EPS)
    u = p0[...].astype(f32)
    for piece in (p1, p2, p3):
        u = u + piece[...].astype(f32)
    u = u * misc_ref[16:17, :].astype(f32)
    out = dresid_ref[...] + rinv * u - xin * (rinv * rinv * rinv) * jnp.mean(u * xin, axis=1, keepdims=True)
    out_ref[...] = out.astype(bf16)


def kernel_block_out(gx_ref, resid_ref, *rest):
    pieces, out_ref = rest[:4], rest[4]
    valid_row = jnp.broadcast_to((gx_ref[TOK + 8 : TOK + 9, :TOK].astype(f32) > 0.5).astype(f32), (TOK, TOK))
    valid = valid_row.T[:, 0:1]
    total = resid_ref[...]
    for piece in pieces:
        total = total + piece[...].astype(f32)
    out_ref[...] = (total * valid).astype(bf16)


def call(body, outs, ins, scratch=(), mib=60, flops=0, nbytes=0, name=None):
    return pl.pallas_call(
        body,
        out_shape=[jax.ShapeDtypeStruct(shape, dtype) for shape, dtype, _ in outs],
        in_specs=[spec for _, spec in ins],
        out_specs=[spec for _, _, spec in outs],
        scratch_shapes=list(scratch),
        compiler_params=params(mib),
        cost_estimate=pl.CostEstimate(flops=flops // 10**4, bytes_accessed=nbytes // 10**4, transcendentals=0),
        name=name,
    )(*[value for value, _ in ins])


def sum_pieces(pieces):
    total = pieces[0].astype(f32)
    for piece in pieces[1:]:
        total = total + piece.astype(f32)
    return total


def all_gather_z(value):
    spread = jnp.broadcast_to(value[None], (4,) + value.shape)
    return lax.all_to_all(spread, "z", split_axis=0, concat_axis=0, tiled=True)


def pick(value, axis, index):
    return lax.dynamic_index_in_dim(value, index, axis, keepdims=False)


def on_device(
    tokens, segment_ids, routes, cotangent, attn_gain, query_weight, key_weight, value_weight,
    output_weight, expert_gain, router_weight, expert_in, expert_out,
):
    V, A, S = spec_vmem(), spec_any(), spec_smem()
    iz, ih, ix, ic, il = [lax.axis_index(name) for name in AX]
    where = jnp.stack([iz, ih, ix, ic, il]).astype(jnp.int32)
    cos_np, sin_np = rope_tables()
    cos_full, sin_full = jnp.asarray(cos_np), jnp.asarray(sin_np)

    ints = jnp.concatenate(
        [routes.reshape(TOK, TOPK).T, segment_ids.reshape(1, TOK), jnp.zeros((7, TOK), jnp.int32)], axis=0
    ).astype(bf16)
    ints = jnp.pad(ints, ((0, 0), (0, D - TOK)))
    x_own = jnp.concatenate([tokens.reshape(TOK, D), ints], axis=0)
    g_own = jnp.concatenate([cotangent.reshape(TOK, D), ints], axis=0)
    small = jnp.concatenate(
        [router_weight, attn_gain[:, None], expert_gain[:, None], jnp.zeros((12, 46), bf16)], axis=1
    )
    heads = jnp.concatenate(
        [
            query_weight.reshape(12, 8, 192),
            key_weight.reshape(12, 8, 64),
            value_weight.reshape(12, 8, 64),
            jnp.broadcast_to(small[:, None, :], (12, 8, 64)),
        ],
        axis=2,
    ).transpose(1, 0, 2)
    heads = jnp.broadcast_to(heads[:, None], (8, 2, 12, QKVM)).reshape(16, 12, QKVM)
    heads = lax.all_to_all(heads, ("z", "c", "yl"), split_axis=0, concat_axis=0, tiled=True)
    heads = heads.reshape(4, 48, QKVM)
    o_in = jnp.stack(
        [output_weight, send(output_weight, dl=1), send(output_weight, dc=1), send(output_weight, dc=1, dl=1)]
    )
    o48 = jnp.take(o_in, (ic * 2 + il) ^ jnp.arange(4), axis=0, mode="clip").reshape(48, D)
    expert_in, heads = lax.optimization_barrier((expert_in, heads))
    heads = jnp.stack([heads, send(heads, dh=1, dl=1)])
    x_z = [x_own] + [send(x_own, dz=j) for j in (1, 2, 3)]
    o48, heads, x_z = lax.optimization_barrier((o48, heads, x_z))
    o48 = jnp.where(ih == ic, o48, send(o48, dh=1, dl=1))
    w_pieces = [heads] + [send(heads, dx=k) for k in (1, 2, 3)]
    o_pieces = [o48] + [send(o48, dx=k) for k in (1, 2, 3)]
    dense = [(p, A) for p in w_pieces + o_pieces]

    x_all = x_z + [send(item, dc=1) for item in x_z]

    g_x = jnp.stack([g_own] + [send(g_own, dx=k) for k in (1, 2, 3)])
    g_xy = [g_x, send(g_x, dl=1)]

    e_out = expert_out.reshape(8, 8, 3, 512).transpose(0, 2, 1, 3).reshape(8, 24, 512)
    e_pack = jnp.concatenate([expert_in, e_out], axis=2)
    e_pack = lax.all_to_all(e_pack, ("x", "c"), split_axis=0, concat_axis=0, tiled=True)
    e_out = e_pack[:, :, 1024:].reshape(8, 3, 8, 512).transpose(1, 0, 2, 3).reshape(192, 512)
    e_pack = jnp.concatenate([e_pack[:, :, :1024].reshape(192, 1024), e_out], axis=1)
    e_full = lax.all_gather(e_pack, ("z", "yh"), axis=0, tiled=True)

    normed, qk_b, v_b, mixed, misc, part_own, part_sib = call(
        kernel_attn,
        [
            ((ROWS, D), bf16, V), ((ROWS, QK), bf16, V), ((ROWS, 128), bf16, V), ((ROWS, HQ), bf16, V),
            ((64, D), bf16, V), ((4, TOK, D), f32, V), ((4, TOK, D), bf16, V),
        ],
        [(where, S), (cos_full, V), (sin_full, V)] + [(p, V) for p in x_all] + dense,
        [
            pltpu.VMEM((D, QKVM), bf16), pltpu.VMEM((HQ, D), bf16),
            pltpu.SemaphoreType.DMA((32,)), pltpu.SemaphoreType.DMA((4,)),
        ],
        flops=2 * ROWS * D * 512, nbytes=12 * 2**20, name="attention",
    )

    def core_sum(own, sib):
        return call(
            kernel_core_sum, [((TOK, D), bf16, V)] * 4, [(own, V), (send(sib, dc=1), V)],
            flops=10**6, nbytes=6 * 2**20, name="core_sum",
        )

    def team_sum(parts):
        return [parts[0]] + [send(parts[j], dz=j) for j in (1, 2, 3)]

    g_all = g_xy + [send(item, dc=1) for item in g_xy]
    attn_pieces = team_sum(core_sum(part_own, part_sib))
    attn_pieces, g_all = lax.optimization_barrier((attn_pieces, g_all))
    resid, n2, gates, n2_a, n2_b = call(
        kernel_resid,
        [
            ((TOK, D), f32, V), ((TOK, D), bf16, V), ((16, TOK), f32, V),
            ((8, SEQ, D), bf16, V), ((8, SEQ, D), bf16, V),
        ],
        [(x_own, V)] + [(p, V) for p in attn_pieces] + [(misc, V)],
        flops=10**7, nbytes=6 * 2**20, name="residual_norm",
    )

    def group_exchange(value):
        return lax.all_to_all(value, ("x", "yl"), split_axis=0, concat_axis=0, tiled=True)

    dn, mix, kept = [], [], []
    group_rows = [group_exchange(n2_a), group_exchange(n2_b)]
    for half, rows in enumerate(group_rows):
        if half:
            rows, _ = lax.optimization_barrier((rows, outs[0]))
        rows_sib = send(rows, dc=1)
        outs = call(
            functools.partial(kernel_expert, half),
            [
                ((8, 80, D), bf16, V), ((8, SEQ, D), bf16, V),
                ((512, D), bf16, V), ((512, D), bf16, V), ((512, F), bf16, V), ((512, 1024), bf16, V),
            ]
            + [((2, 80, D), bf16, V)] * 4
            + [((2, SEQ, D), bf16, V)] * 4,
            [(where, S), (misc, V), (rows, A), (rows_sib, A), (e_full, A)] + [(p, A) for p in g_all],
            [
                pltpu.VMEM((16, SEQ, D), bf16), pltpu.VMEM((16, 80, D), bf16),
                pltpu.VMEM((D, 1024), bf16), pltpu.VMEM((F, D), bf16),
                pltpu.VMEM((16, SEQ), f32), pltpu.VMEM((16, SEQ), f32), pltpu.VMEM((16, 1024), f32),
                pltpu.SemaphoreType.DMA((2,)), pltpu.SemaphoreType.DMA((32,)), pltpu.SemaphoreType.DMA((32,)),
            ],
            flops=6 * 10**9, nbytes=30 * 2**20, name="experts",
        )
        recv = [send(v, dc=1) for v in outs[6:10]]
        if half:
            recv, dn[0] = lax.optimization_barrier((recv, dn[0]))
        (summed,) = call(
            kernel_pair_sum, [((8, 80, D), bf16, V)], [(outs[0], V)] + [(v, V) for v in recv],
            flops=10**7, nbytes=6 * 2**20, name="pair_sum",
        )
        dn.append(group_exchange(summed))
        mix.append((outs[1], outs[10:14]))
        kept.extend(outs[2:6])
    kept[0], _ = lax.optimization_barrier((kept[0], summed))
    (e_grad,) = call(
        kernel_expert_grads, [((D, D), bf16, V)], [(v, V) for v in kept],
        flops=6 * 10**9, nbytes=14 * 2**20, name="expert_gradients",
    )
    mix[1], _ = lax.optimization_barrier((mix[1], e_grad))
    mix_sums = [(v, V) for own, sib in mix for v in [own] + [send(piece, dc=1) for piece in sib]]
    mix_sum = call(
        kernel_mix_sum, [((4, TOK, D), bf16, V)] * 2, [(where, S)] + mix_sums,
        flops=10**7, nbytes=10 * 2**20, name="mix_sum",
    )
    dn[1], e_grad, mix_sum = lax.optimization_barrier((dn[1], e_grad, mix_sum))
    e_sum = lax.psum_scatter(e_grad, ("z", "yh"), scatter_dimension=0, tiled=True)
    dresid, dattn, small_grad = call(
        kernel_home,
        [((TOK, D), f32, V), ((TOK, D), bf16, V), ((32, D), f32, V)],
        [(g_own, V), (resid, V), (n2, V), (gates, V), (misc, V), (dn[0], V), (dn[1], V)],
        [pltpu.VMEM((16, TOK), f32)],
        flops=10**8, nbytes=6 * 2**20, name="home_gradient",
    )
    da_z = [dattn] + [send(dattn, dz=j) for j in (1, 2, 3)]
    da_all = da_z + [send(item, dc=1) for item in da_z]
    mix_keep, mix_give = mix_sum
    mix_recv = send(mix_give, dl=1)
    da_all, mix_recv = lax.optimization_barrier((da_all, mix_recv))
    outs = call(
        kernel_back,
        [((4, TOK, D), f32, V), ((4, TOK, D), bf16, V)]
        + [((2, 4, 48, QKVM), bf16, A)] * 4
        + [((48, D), bf16, A)] * 4,
        [
            (where, S), (normed, V), (qk_b, V), (v_b, V), (mixed, V), (small_grad, V), (cos_full, V), (sin_full, V),
        ]
        + [(p, V) for p in x_all + da_all]
        + dense,
        [
            pltpu.VMEM((D, QKVM), bf16), pltpu.VMEM((HQ, D), bf16), pltpu.VMEM((ROWS, D), bf16),
            pltpu.VMEM((ROWS, HQ), bf16), pltpu.VMEM((ROWS, QK), f32), pltpu.VMEM((ROWS, QKVM), bf16),
            pltpu.VMEM((D, QKVM), bf16), pltpu.VMEM((HQ, D), bf16),
            pltpu.SemaphoreType.DMA((32,)), pltpu.SemaphoreType.DMA((4,)), pltpu.SemaphoreType.DMA((36,)),
        ],
        flops=6 * ROWS * D * 512, nbytes=20 * 2**20, name="attention_back",
    )
    dn1_own, dn1_sib = outs[:2]
    wg, og = outs[2:6], outs[6:10]
    wg = [wg[0]] + [send(wg[k], dx=k) for k in (1, 2, 3)]
    og = [og[0]] + [send(og[k], dx=k) for k in (1, 2, 3)]
    dn1_parts = core_sum(dn1_own, dn1_sib)
    wg, og, dn1_parts = lax.optimization_barrier((wg, og, dn1_parts))
    (token_grad,) = call(
        kernel_token_grad, [((TOK, D), bf16, V)],
        [(x_own, V), (dresid, V)] + [(p, V) for p in team_sum(dn1_parts)] + [(misc, V)],
        flops=10**7, nbytes=3 * 2**20, name="token_gradient",
    )
    ge_out = e_sum[:, 1024:].reshape(3, 8, 8, 512).transpose(1, 0, 2, 3).reshape(8, 24, 512)
    ge = jnp.concatenate([e_sum[:, :1024].reshape(8, 24, 1024), ge_out], axis=2)
    ge = lax.all_to_all(ge, ("x", "c"), split_axis=0, concat_axis=0, tiled=True).astype(f32)
    ge_in = ge[:, :, :1024]
    ge_out = ge[:, :, 1024:].reshape(8, 3, 8, 512).transpose(0, 2, 1, 3).reshape(8, 8, D)

    mix_pieces = call(
        kernel_mix_pair, [((TOK, D), bf16, V)] * 4,
        [(where, S), (mix_keep, V), (mix_recv, V)],
        flops=10**6, nbytes=5 * 2**20, name="mix_pair",
    )
    mix_pieces = [mix_pieces[0]] + [send(mix_pieces[k], dx=k) for k in (1, 2, 3)]
    (block_out,) = call(
        kernel_block_out, [((TOK, D), bf16, V)], [(g_own, V), (resid, V)] + [(p, V) for p in mix_pieces],
        flops=10**7, nbytes=5 * 2**20, name="block_output",
    )

    w_keep, w_give, o_keep, o_give = call(
        kernel_dense_sum,
        [((4, 48, QKVM), bf16, V)] * 2 + [((48, D), bf16, V)] * 2,
        [(where, S)] + [(v, V) for v in wg + og],
        flops=10**6, nbytes=5 * 2**20, name="dense_sum",
    )
    heads = (w_keep.astype(f32) + send(w_give, dh=1, dl=1).astype(f32)).astype(bf16).reshape(16, 12, QKVM)
    heads = lax.all_to_all(heads, ("z", "c", "yl"), split_axis=0, concat_axis=0, tiled=True).astype(f32)
    heads = heads.reshape(8, 2, 12, QKVM).sum(axis=1)
    back = (o_keep.astype(f32) + send(o_give, dh=1, dl=1).astype(f32)).astype(bf16).reshape(4, 12, D)
    me = ic * 2 + il
    d_o = pick(back, 0, me).astype(f32) + send(pick(back, 0, me ^ 1), dl=1).astype(f32)
    d_o = d_o + send(pick(back, 0, me ^ 2), dc=1).astype(f32) + send(pick(back, 0, me ^ 3), dc=1, dl=1).astype(f32)
    dq = heads[:, :, :HQ].transpose(1, 0, 2).reshape(12, D)
    dk = heads[:, :, HQ:QK].transpose(1, 0, 2).reshape(12, 512)
    dv = heads[:, :, QK:QKV].transpose(1, 0, 2).reshape(12, 512)
    d_small = heads[:, :, QKV:].sum(axis=0)
    return (
        block_out.reshape(2, SEQ, D),
        token_grad.reshape(2, SEQ, D),
        d_small[:, 16],
        dq,
        dk,
        dv,
        d_o,
        d_small[:, 17],
        d_small[:, :16],
        ge_in,
        ge_out,
    )


def solution(mesh):
    devices = mesh.devices.reshape(DIMS) if hasattr(mesh, "devices") else None
    fine = Mesh(devices, AX)
    every = ("z", "yh", "x", "c", "yl")
    dp = ("z", "yh", "x", "c")
    in_specs = (
        P(every, None, None), P(every, None), P(every, None, None), P(every, None, None), P(every),
        P(every, None), P(every, None), P(every, None), P(every, None), P(every), P(every, None),
        P("yl", dp, None), P("yl", dp, None),
    )
    out_specs = (
        P(every, None, None), P(every, None, None), P(every), P(every, None), P(every, None),
        P(every, None), P(every, None), P(every), P(every, None), P("yl", dp, None), P("yl", dp, None),
    )
    return jax.shard_map(on_device, mesh=fine, in_specs=in_specs, out_specs=out_specs, check_vma=False)
```

```python
import functools

import jax
import jax.numpy as jnp
import numpy as np
from jax import lax
from jax.experimental import pallas as pl
from jax.experimental.pallas import tpu as pltpu
from jax.sharding import Mesh
from jax.sharding import PartitionSpec as P

D = 1536
Q_HEADS = 24
KV_HEADS = 8
HEAD_DIM = 64
F = 512
TOPK = 8
EXPERTS = 16
SEQ = 64
CAP = 32

AX = ("z", "yh", "x", "c", "yl")
DIMS = (4, 2, 4, 2, 2)
EPS = 1e-5
NEG = -1e30
TOK = 128
EXT = 144
HQ = 192
QK = 256
QKV = 320
QKVM = 384
WIDE = 640
ROWS = 1024
bf16 = jnp.bfloat16
f32 = jnp.float32


def coords_list():
    return list(np.ndindex(*DIMS))


def send(value, dz=0, dh=0, dx=0, dc=0, dl=0):
    flat = {pos: i for i, pos in enumerate(coords_list())}
    pairs = [
        (i, flat[(z ^ dz, h ^ dh, x ^ dx, c ^ dc, l ^ dl)])
        for (z, h, x, c, l), i in flat.items()
    ]
    return lax.ppermute(value, AX, pairs)


def dot(a, b):
    return jnp.dot(a, b, preferred_element_type=f32)


def dot_t(a, b):
    return lax.dot_general(a, b, (((1,), (1,)), ((), ())), preferred_element_type=f32)


def t_dot(a, b):
    return lax.dot_general(a, b, (((0,), (0,)), ((), ())), preferred_element_type=f32)


def params(mib=60):
    return pltpu.CompilerParams(vmem_limit_bytes=mib * 2**20)


def rope_tables():
    angle = np.arange(SEQ)[:, None] * (10000.0 ** (-np.arange(32) * 2.0 / 64))[None, :]
    cosine, sine = np.cos(angle), np.sin(angle)
    cos_full = np.concatenate([cosine, cosine] * 2, axis=1)
    sin_full = np.concatenate([-sine, sine] * 2, axis=1)
    return np.tile(cos_full, (4, 1)).astype(np.float32), np.tile(sin_full, (4, 1)).astype(np.float32)


def turn(values, cos_full, sin_full):
    width = values.shape[1]
    lane = lax.broadcasted_iota(jnp.int32, values.shape, 1)
    ahead = pltpu.roll(values, width - 32, 1)
    behind = pltpu.roll(values, 32, 1)
    partner = jnp.where((lane % 64) < 32, ahead, behind)
    copies = width // 128
    cos_wide = jnp.concatenate([cos_full] * copies, axis=1)
    sin_wide = jnp.concatenate([sin_full] * copies, axis=1)
    return values * cos_wide + partner * sin_wide


def allowed_mask(ints):
    row = jnp.broadcast_to(ints[8:9, :], (TOK, TOK))
    col = row.T
    p = lax.broadcasted_iota(jnp.int32, (TOK, TOK), 0)
    t = lax.broadcasted_iota(jnp.int32, (TOK, TOK), 1)
    return (row == col) & (t <= p) & ((p < SEQ) == (t < SEQ))


def qkv_copies(pieces, target, sems, h, x):
    copies = []
    for k in range(4):
        for b in range(2):
            for zz in range(4):
                start = pl.multiple_of(((zz * 2 + (h ^ b)) * 4 + (x ^ k)) * 48, 16)
                copies.append(
                    pltpu.make_async_copy(
                        pieces[k].at[b, zz, :, pl.ds(0, QKVM)],
                        target.at[pl.ds(start, 48), :],
                        sems.at[(k * 2 + b) * 4 + zz],
                    )
                )
    return copies


def o_copies(pieces, target, sems, x):
    copies = []
    for k in range(4):
        for q in range(6):
            start = pl.multiple_of((x ^ k) * 48, 16)
            copies.append(
                pltpu.make_async_copy(
                    pieces[k].at[q // 4, q % 4, :, pl.ds(QKVM, 256)],
                    target.at[pl.ds(start, 48), pl.ds(256 * q, 256)],
                    sems.at[k * 6 + q],
                )
            )
    return copies


def spec_any():
    return pl.BlockSpec(memory_space=pl.ANY)


def spec_vmem():
    return pl.BlockSpec(memory_space=pltpu.VMEM)


def spec_smem():
    return pl.BlockSpec(memory_space=pltpu.SMEM)


def unit(size):
    row = lax.broadcasted_iota(jnp.int32, (size, size), 0)
    return (row == lax.broadcasted_iota(jnp.int32, (size, size), 1)).astype(f32).astype(bf16)


def kernel_attn(where, cos_ref, sin_ref, x_own, x_sib, *rest):
    x_in = [x_own.at[j] for j in range(4)] + [x_sib.at[j] for j in range(4)]
    w_in = rest[:4]
    normed_ref, qk_ref, v_ref, mixed_ref, misc_ref, own_ref, sib_ref = rest[4:11]
    w, wo, sems, osems = rest[11:]
    copies = qkv_copies(w_in, w, sems, where[1], where[2])
    more = o_copies(w_in, wo, osems, where[2])
    for item in copies + more:
        item.start()
    for item in copies:
        item.wait()
    misc = dot_t(unit(64), w[:, QKV:])
    misc_ref[...] = misc.astype(bf16)
    gain = misc[16:17, :]
    for m in range(8):
        rows = slice(m * TOK, (m + 1) * TOK)
        xin = x_in[m][0:TOK, :].astype(f32)
        rinv = lax.rsqrt(jnp.mean(xin * xin, axis=1, keepdims=True) + EPS)
        normed_ref[rows, :] = (xin * rinv * gain).astype(bf16)
    cos_full, sin_full = cos_ref[...], sin_ref[...]
    for m in range(4):
        rows = slice(m * 256, (m + 1) * 256)
        qkv = dot(normed_ref[rows, :], w[:, 0:QKVM])
        qk_ref[rows, :] = turn(qkv[:, 0:QK], cos_full, sin_full).astype(bf16)
        v_ref[rows, :] = qkv[:, QK:QKVM].astype(bf16)
    for m in range(8):
        ok = allowed_mask(x_in[m][TOK:EXT, :TOK].astype(f32))
        ok3 = jnp.concatenate([ok.astype(f32)] * 3, axis=0) > 0.5
        rows = slice(m * TOK, (m + 1) * TOK)
        keys = qk_ref[rows, HQ:QK]
        vals = v_ref[rows, 0:64]
        q3 = jnp.concatenate([qk_ref[rows, g * 64 : (g + 1) * 64] for g in range(3)], axis=0)
        scores = jnp.where(ok3, dot_t(q3, keys) * 0.125, NEG)
        top = jnp.max(scores, axis=1, keepdims=True)
        expo = jnp.exp(scores - top)
        probs = (expo / jnp.sum(expo, axis=1, keepdims=True)).astype(bf16)
        out = dot(probs, vals).astype(bf16)
        for g in range(3):
            mixed_ref[rows, g * 64 : (g + 1) * 64] = out[g * TOK : (g + 1) * TOK, :]
    for item in more:
        item.wait()
    for m in range(4):
        rows = slice(m * TOK, (m + 1) * TOK)
        own_ref[m] = dot(mixed_ref[rows, :], wo[...])
        rows = slice((4 + m) * TOK, (5 + m) * TOK)
        sib_ref[m] = dot(mixed_ref[rows, :], wo[...]).astype(bf16)


def kernel_core_sum(own_ref, recv_ref, *outs):
    for m in range(4):
        outs[m][...] = (own_ref[m] + recv_ref[m].astype(f32)).astype(bf16)


def kernel_core_sum_z(where, own_ref, recv_ref, out_ref):
    for m in range(4):
        out_ref[where[0] ^ m] = (own_ref[m] + recv_ref[m].astype(f32)).astype(bf16)


def chosen_gates(misc, n2, ints):
    logits = dot_t(misc, n2)
    expert = lax.broadcasted_iota(jnp.int32, logits.shape, 0).astype(f32)
    hot = jnp.zeros(logits.shape, f32)
    for k in range(TOPK):
        hot = jnp.maximum(hot, (expert == ints[k : k + 1, :]).astype(f32))
    masked = jnp.where(hot > 0.5, logits, NEG)
    expo = jnp.where(hot > 0.5, jnp.exp(masked - jnp.max(masked, axis=0, keepdims=True)), 0.0)
    return expo / jnp.sum(expo, axis=0, keepdims=True)


def kernel_resid(xo, parts, misc_ref, resid_ref, n2_ref, gates_ref, na_ref, nb_ref):
    resid = xo[:TOK, :].astype(f32)
    for m in range(4):
        resid = resid + parts[m].astype(f32)
    resid_ref[...] = resid
    rinv = lax.rsqrt(jnp.mean(resid * resid, axis=1, keepdims=True) + EPS)
    n2 = (resid * rinv * misc_ref[17:18, :].astype(f32)).astype(bf16)
    n2_ref[...] = n2
    for m in range(8):
        na_ref[m] = n2[:SEQ, :]
        nb_ref[m] = n2[SEQ:, :]
    gates_ref[...] = chosen_gates(misc_ref[0:16, :], n2, xo[TOK:EXT, :TOK].astype(f32))


def kernel_expert(half, where, misc_ref, n2_own, n2_sib, w_ref, *rest):
    gx_in = rest[:8]
    dn_own, mix_own, disp_out, dslot_out, hid_out, dgu_out = rest[8:14]
    dn_sib, mix_sib = rest[14:18], rest[18]
    (n2, gx, win, wout, slot_s, gate_s, ints_s, disp, dslot, hid, dgu, dn_s, mix_s,
     n2_sem, gx_sem, w_sem, out_sem) = rest[19:]
    x, c, l = where[2], where[3], where[4]
    me = (l * 8 + x * 2 + c).astype(f32)
    w_copies = []
    for blk in range(8):
        w_copies.append(
            pltpu.make_async_copy(
                w_ref.at[pl.ds(blk * 192, 192), pl.ds(0, 1024)], win.at[pl.ds(blk * 192, 192), :], w_sem.at[blk * 4]
            )
        )
        for t in range(3):
            w_copies.append(
                pltpu.make_async_copy(
                    w_ref.at[pl.ds(blk * 192 + 64 * t, 64), pl.ds(1024, 512)],
                    wout.at[pl.ds(blk * 64, 64), pl.ds(512 * t, 512)],
                    w_sem.at[blk * 4 + 1 + t],
                )
            )
    n2_copies = [
        pltpu.make_async_copy(n2_own, n2.at[pl.ds(0, 8)], n2_sem.at[0]),
        pltpu.make_async_copy(n2_sib, n2.at[pl.ds(8, 8)], n2_sem.at[1]),
    ]
    gx_copies = []
    for core in range(2):
        for k in range(4):
            for b in range(2):
                at = core * 8 + (x ^ k) * 2 + (l ^ b)
                g_src = gx_in[core * 4 + k].at[b]
                gx_copies.append(
                    pltpu.make_async_copy(
                        g_src.at[pl.ds(SEQ * half, SEQ), :], gx.at[at, pl.ds(0, SEQ), :], gx_sem.at[(core * 8 + k * 2 + b) * 2]
                    )
                )
                gx_copies.append(
                    pltpu.make_async_copy(
                        g_src.at[pl.ds(TOK, 16), :], gx.at[at, pl.ds(SEQ, 16), :], gx_sem.at[(core * 8 + k * 2 + b) * 2 + 1]
                    )
                )
    for item in gx_copies + n2_copies + w_copies:
        item.start()
    for item in gx_copies + n2_copies:
        item.wait()
    for m in range(16):
        ints_s[:, SEQ * m : SEQ * (m + 1)] = gx[m, SEQ : SEQ + 16, SEQ * half : SEQ * (half + 1)].astype(f32)
    token = lax.broadcasted_iota(jnp.int32, (TOK, TOK), 0)
    after = lax.broadcasted_iota(jnp.int32, (TOK, TOK), 1)
    before = ((token < after) & ((token < SEQ) == (after < SEQ))).astype(f32).astype(bf16)
    for core in range(2):
        lanes = slice(core * 512, core * 512 + 512)
        ints = ints_s[:, lanes]
        gates = chosen_gates(misc_ref[0:16, :], n2[8 * core : 8 * core + 8].reshape(512, D), ints)
        expert = lax.broadcasted_iota(jnp.int32, gates.shape, 0).astype(f32)
        gate = jnp.sum(jnp.where(expert == me, gates, 0.0), axis=0, keepdims=True)
        hit = jnp.max((ints[0:8, :] == me).astype(f32), axis=0, keepdims=True)
        hit = hit * (ints[8:9, :] > 0.5).astype(f32)
        rank = jnp.concatenate(
            [
                dot(jnp.broadcast_to(hit[:, u * TOK : (u + 1) * TOK], (16, TOK)).astype(bf16), before)[0:1, :]
                for u in range(4)
            ],
            axis=1,
        )
        slot = jnp.where((hit > 0.5) & (rank < CAP - 0.5), rank, -1.0)
        for q in range(8):
            slot_s[core * 8 + q : core * 8 + q + 1, :] = slot[:, q * SEQ : (q + 1) * SEQ]
            gate_s[core * 8 + q : core * 8 + q + 1, :] = gate[:, q * SEQ : (q + 1) * SEQ]
    slot_iota = lax.broadcasted_iota(jnp.int32, (CAP, SEQ), 0).astype(f32)
    line = lax.broadcasted_iota(jnp.int32, (16, SEQ), 0)
    going = []

    def give(src, dst):
        copy = pltpu.make_async_copy(src, dst, out_sem.at[len(going)])
        copy.start()
        going.append(copy)

    for i in range(2):
        rows = slice(i * 256, (i + 1) * 256)
        hots, gate_cols, g_parts = [], [], []
        for q in range(8):
            m = i * 8 + q
            hot = (slot_iota == slot_s[m : m + 1, :]).astype(f32)
            gate_col = jnp.sum(hot * gate_s[m : m + 1, :], axis=1, keepdims=True)
            hot_b = hot.astype(bf16)
            hots.append(hot_b)
            gate_cols.append(gate_col)
            srows = slice(i * 256 + q * CAP, i * 256 + (q + 1) * CAP)
            disp[srows, :] = dot(hot_b, n2[m]).astype(bf16)
            gsl = dot(hot_b, gx[m, 0:SEQ, :])
            g_parts.append(gsl)
            dslot[srows, :] = (gate_col * gsl).astype(bf16)
        give(disp.at[rows, :], disp_out.at[rows, :])
        give(dslot.at[rows, :], dslot_out.at[rows, :])
        if i == 0:
            for item in w_copies:
                item.wait()
        gup = dot(disp[rows, :], win[...])
        gate_part, up_part = gup[:, :F], gup[:, F:]
        sig = jax.nn.sigmoid(gate_part)
        hidden = (gate_part * sig * up_part).astype(bf16)
        hid[rows, :] = hidden
        give(hid.at[rows, :], hid_out.at[rows, :])
        dhid = dot_t(dslot[rows, :], wout[...])
        silu_grad = sig * (1.0 + gate_part * (1.0 - sig))
        dg = jnp.concatenate([dhid * up_part * silu_grad, dhid * gate_part * sig], axis=1).astype(bf16)
        dgu[rows, :] = dg
        give(dgu.at[rows, :], dgu_out.at[rows, :])
        out_rows = dot(hidden, wout[...]).astype(bf16).astype(f32)
        for q in range(8):
            part = slice(q * CAP, (q + 1) * CAP)
            m = i * 8 + q
            dgate = jnp.sum(g_parts[q] * out_rows[part, :], axis=1, keepdims=True)
            dgate_row = jnp.sum(hots[q].astype(f32) * dgate, axis=0, keepdims=True)
            high = dgate_row.astype(bf16).astype(f32)
            low = dgate_row - high
            extra = jnp.where(line == 2 * c, high, 0.0) + jnp.where(line == 2 * c + 1, low, 0.0)
            dn_s[m, SEQ : SEQ + 16, :] = jnp.zeros((16, D), bf16)
            dn_s[m, SEQ : SEQ + 16, 0:SEQ] = extra.astype(bf16)
            weighted = (gate_cols[q] * out_rows[part, :]).astype(bf16)
            mix_s[m, :, :] = t_dot(hots[q], weighted).astype(bf16)
        if i == 0:
            give(mix_s.at[pl.ds(0, 8)], mix_own)
        else:
            give(mix_s.at[pl.ds(8, 8)], mix_sib)
        din = dot_t(dg, win[...]).astype(bf16)
        for q in range(8):
            dn_s[i * 8 + q, 0:SEQ, :] = t_dot(hots[q], din[q * CAP : (q + 1) * CAP, :]).astype(bf16)
        if i == 0:
            give(dn_s.at[pl.ds(0, 8)], dn_own)
        else:
            for k in range(4):
                give(dn_s.at[pl.ds(8 + 2 * k, 2)], dn_sib[k])
    for copy in going:
        copy.wait()


def kernel_expert_grads(disp_a, dslot_a, hid_a, dgu_a, disp_b, dslot_b, hid_b, dgu_b, wg):
    for n in range(6):
        cols = slice(n * 256, (n + 1) * 256)
        wg[cols, 0:1024] = (t_dot(disp_a[:, cols], dgu_a[...]) + t_dot(disp_b[:, cols], dgu_b[...])).astype(bf16)
    for n in range(2):
        cols = slice(n * 256, (n + 1) * 256)
        out_g = (t_dot(hid_a[:, cols], dslot_a[...]) + t_dot(hid_b[:, cols], dslot_b[...])).astype(bf16)
        for b in range(4):
            blk = n * 4 + b
            for t in range(3):
                wg[blk * 192 + t * 64 : blk * 192 + (t + 1) * 64, 1024:1536] = out_g[
                    b * 64 : (b + 1) * 64, t * 512 : (t + 1) * 512
                ]


def kernel_pair_sum(*refs):
    out = refs[-1]
    lines = 0
    for i in range(0, len(refs) - 1, 5):
        size = refs[i].shape[1]
        for m in range(8):
            total = refs[i][m].astype(f32) + refs[i + 1 + m // 2][m % 2].astype(f32)
            out[m, lines : lines + size, :] = total.astype(bf16)
        lines += size


def kernel_mix_sum(where, own_a, sib_a, own_b, sib_b, *outs):
    for half, (own, sib) in enumerate(((own_a, sib_a), (own_b, sib_b))):
        for k in range(4):
            for ll in range(2):
                m = (where[2] ^ k) * 2 + ll
                outs[half * 4 + k][ll] = (own[m].astype(f32) + sib[m].astype(f32)).astype(bf16)


def kernel_mix_pair(where, *refs):
    l = where[4]
    for out, line in ((refs[8], l), (refs[9], 1 - l)):
        for half in range(2):
            total = refs[half * 4][line].astype(f32)
            for k in range(1, 4):
                total = total + refs[half * 4 + k][line].astype(f32)
            out[SEQ * half : SEQ * (half + 1), :] = total.astype(bf16)


def kernel_home(gx_ref, resid_ref, n2_ref, gates_ref, misc_ref, dn_a, dn_b, dresid_ref, dattn_ref, small_ref, dg_s):
    for xx in range(4):
        for ll in range(2):
            for half, dn in enumerate((dn_a, dn_b)):
                extra = dn[xx * 2 + ll, SEQ : SEQ + 16, 0:SEQ].astype(f32)
                first = ll * 8 + xx * 2
                lanes = slice(SEQ * half, SEQ * (half + 1))
                dg_s[first : first + 1, lanes] = extra[0:1, :] + extra[1:2, :]
                dg_s[first + 1 : first + 2, lanes] = extra[2:3, :] + extra[3:4, :]
    gates = gates_ref[...]
    dgates = dg_s[...]
    dlog = (gates * (dgates - jnp.sum(gates * dgates, axis=0, keepdims=True))).astype(bf16)
    valid_row = jnp.broadcast_to((gx_ref[TOK + 8 : TOK + 9, :TOK].astype(f32) > 0.5).astype(f32), (TOK, TOK))
    valid = valid_row.T[:, 0:1]
    total = t_dot(dlog, misc_ref[0:16, :])
    sums = []
    for dn in (dn_a, dn_b):
        part = dn[0, 0:SEQ, :].astype(f32)
        for m in range(1, 8):
            part = part + dn[m, 0:SEQ, :].astype(f32)
        sums.append(part)
    total = total + jnp.concatenate(sums, axis=0)
    resid = resid_ref[...]
    rinv = lax.rsqrt(jnp.mean(resid * resid, axis=1, keepdims=True) + EPS)
    u = total * misc_ref[17:18, :].astype(f32)
    g = gx_ref[0:TOK, :].astype(f32) * valid
    dresid = g + rinv * u - resid * (rinv * rinv * rinv) * jnp.mean(u * resid, axis=1, keepdims=True)
    dresid_ref[...] = dresid
    for m in range(4):
        dattn_ref[m] = dresid.astype(bf16)
    small_ref[0:16, :] = dot(dlog, n2_ref[...])
    gain = jnp.sum(total * resid * rinv, axis=0, keepdims=True)
    line = lax.broadcasted_iota(jnp.int32, (16, D), 0)
    small_ref[16:32, :] = jnp.where(line == 1, gain, 0.0)


def kernel_back(
    where, normed_ref, qk_ref, v_ref, mixed_ref, small_ref, cos_ref, sin_ref, x_own, x_sib, da_own, da_sib, *rest
):
    da_in = [da_own.at[where[0] ^ j] for j in range(4)] + [da_sib.at[where[0] ^ j] for j in range(4)]
    w_in = rest[:4]
    w_out, dcat = rest[4:6]
    w, wo, da, dmixed, dqk, wg, og, ints, sems, osems, gsems, isems = rest[6:]
    h, x = where[1], where[2]
    o_in = o_copies(w_in, wo, osems, x)
    copies = qkv_copies(w_in, w, sems, h, x)
    marks = [
        pltpu.make_async_copy(
            (x_own, x_sib)[m // 4].at[m % 4, pl.ds(TOK, 16), pl.ds(0, TOK)], ints.at[m], isems.at[m]
        )
        for m in range(8)
    ]
    for item in marks + o_in + copies:
        item.start()
    for m in range(8):
        da[m * TOK : (m + 1) * TOK, :] = da_in[m][...]
    for item in o_in:
        item.wait()
    for m in range(4):
        rows = slice(m * 256, (m + 1) * 256)
        dmixed[rows, :] = dot_t(da[rows, :], wo[...]).astype(bf16)
    for item in marks:
        item.wait()
    for m in range(8):
        ok = allowed_mask(ints[m].astype(f32))
        ok3 = jnp.concatenate([ok.astype(f32)] * 3, axis=0) > 0.5
        rows = slice(m * TOK, (m + 1) * TOK)
        keys = qk_ref[rows, HQ:QK]
        vals = v_ref[rows, 0:64]
        q3 = jnp.concatenate([qk_ref[rows, g * 64 : (g + 1) * 64] for g in range(3)], axis=0)
        dm3 = jnp.concatenate([dmixed[rows, g * 64 : (g + 1) * 64] for g in range(3)], axis=0)
        scores = jnp.where(ok3, dot_t(q3, keys) * 0.125, NEG)
        top = jnp.max(scores, axis=1, keepdims=True)
        expo = jnp.exp(scores - top)
        probs = expo / jnp.sum(expo, axis=1, keepdims=True)
        dprobs = dot_t(dm3, vals)
        dcat[rows, QK:QKV] = t_dot(probs.astype(bf16), dm3).astype(bf16)
        ds = (probs * (dprobs - jnp.sum(probs * dprobs, axis=1, keepdims=True))).astype(bf16)
        dq3 = dot(ds, keys) * 0.125
        for g in range(3):
            dqk[rows, g * 64 : (g + 1) * 64] = dq3[g * TOK : (g + 1) * TOK, :]
        dqk[rows, HQ:QK] = t_dot(ds, q3) * 0.125
    cos_full, sin_full = cos_ref[...], -sin_ref[...]
    for m in range(4):
        rows = slice(m * 256, (m + 1) * 256)
        dcat[rows, 0:QK] = turn(dqk[rows, :], cos_full, sin_full).astype(bf16)
    dcat[:, QKV:] = jnp.zeros((ROWS, QKVM - QKV), bf16)
    for item in copies:
        item.wait()
    og[:, 0:D] = t_dot(mixed_ref[...], da[...]).astype(bf16)
    og[:, D:] = jnp.zeros((HQ, 512), bf16)
    small = jnp.concatenate([small_ref[...], jnp.zeros((32, D), f32)], axis=0).astype(bf16)
    column = lax.broadcasted_iota(jnp.int32, (256, QKVM - QKV), 1)
    for n in range(6):
        rows = slice(n * 256, (n + 1) * 256)
        grad = t_dot(normed_ref[:, rows], dcat[...])
        gain = jnp.sum(grad[:, 0:QKV] * w[rows, 0:QKV].astype(f32), axis=1, keepdims=True)
        gain = gain / w[rows, QKV + 16 : QKV + 17].astype(f32)
        wg[rows, 0:QKV] = grad[:, 0:QKV].astype(bf16)
        wg[rows, QKV:] = (t_dot(small[:, rows], unit(64)) + jnp.where(column == 16, gain, 0.0)).astype(bf16)
    outs = []
    for k in range(4):
        for b in range(2):
            for zz in range(4):
                start = pl.multiple_of(((zz * 2 + (h ^ b)) * 4 + (x ^ k)) * 48, 16)
                outs.append(
                    pltpu.make_async_copy(
                        wg.at[pl.ds(start, 48), :],
                        w_out.at[x ^ k, b, zz, :, pl.ds(0, QKVM)],
                        gsems.at[(k * 2 + b) * 4 + zz],
                    )
                )
        for q in range(8):
            start = pl.multiple_of((x ^ k) * 48, 16)
            outs.append(
                pltpu.make_async_copy(
                    og.at[pl.ds(start, 48), pl.ds(256 * q, 256)],
                    w_out.at[x ^ k, q // 4, q % 4, :, pl.ds(QKVM, 256)],
                    gsems.at[32 + k * 8 + q],
                )
            )
    for item in outs:
        item.start()
    for item in outs:
        item.wait()


def kernel_back_tokens(where, dcat_ref, *rest):
    w_in, own_ref, sib_ref, w, sems = rest[:4], rest[4], rest[5], rest[6], rest[7]
    copies = qkv_copies(w_in, w, sems, where[1], where[2])
    for item in copies:
        item.start()
    for item in copies:
        item.wait()
    w[:, QKV:] = jnp.zeros((D, QKVM - QKV), bf16)
    for m in range(4):
        own_ref[m] = dot_t(dcat_ref[m * TOK : (m + 1) * TOK, :], w[...])
        sib_ref[m] = dot_t(dcat_ref[(4 + m) * TOK : (5 + m) * TOK, :], w[...]).astype(bf16)


def kernel_dense_sum(where, *refs):
    w_in, outs = [refs[0].at[k] for k in range(4)], refs[1:3]
    here = where[1] == where[3]

    def total(b, zz, lanes):
        out = w_in[0][b, zz, :, lanes].astype(f32)
        for k in range(1, 4):
            out = out + w_in[k][b, zz, :, lanes].astype(f32)
        return out

    for b in range(2):
        for zz in range(4):
            outs[b][zz, :, 0:QKVM] = total(b, zz, slice(0, QKVM)).astype(bf16)
    for q in range(6):
        block = total(q // 4, q % 4, slice(QKVM, WIDE))
        for part in range(2):
            at = q * 2 + part
            lanes = slice(QKVM + 128 * (at % 3), QKVM + 128 * (at % 3 + 1))
            piece = block[:, 128 * part : 128 * (part + 1)]
            outs[0][at // 3, :, lanes] = jnp.where(here, piece, 0.0).astype(bf16)
            outs[1][at // 3, :, lanes] = jnp.where(here, 0.0, piece).astype(bf16)


def kernel_token_grad(xo, dresid_ref, p0, p1, p2, p3, misc_ref, out_ref):
    xin = xo[:TOK, :].astype(f32)
    rinv = lax.rsqrt(jnp.mean(xin * xin, axis=1, keepdims=True) + EPS)
    u = p0[...].astype(f32)
    for piece in (p1, p2, p3):
        u = u + piece[...].astype(f32)
    u = u * misc_ref[16:17, :].astype(f32)
    out = dresid_ref[...] + rinv * u - xin * (rinv * rinv * rinv) * jnp.mean(u * xin, axis=1, keepdims=True)
    out_ref[...] = out.astype(bf16)


def kernel_block_out(gx_ref, resid_ref, *rest):
    pieces, out_ref = rest[:2], rest[2]
    valid_row = jnp.broadcast_to((gx_ref[TOK + 8 : TOK + 9, :TOK].astype(f32) > 0.5).astype(f32), (TOK, TOK))
    valid = valid_row.T[:, 0:1]
    total = resid_ref[...]
    for piece in pieces:
        total = total + piece[...].astype(f32)
    out_ref[...] = (total * valid).astype(bf16)


def call(body, outs, ins, scratch=(), mib=60, flops=0, nbytes=0, name=None):
    return pl.pallas_call(
        body,
        out_shape=[jax.ShapeDtypeStruct(shape, dtype) for shape, dtype, _ in outs],
        in_specs=[spec for _, spec in ins],
        out_specs=[spec for _, _, spec in outs],
        scratch_shapes=list(scratch),
        compiler_params=params(mib),
        cost_estimate=pl.CostEstimate(flops=flops // 10**4, bytes_accessed=nbytes // 10**4, transcendentals=0),
        name=name,
    )(*[value for value, _ in ins])


def pick(value, axis, index):
    return lax.dynamic_index_in_dim(value, index, axis, keepdims=False)


def on_device(
    tokens, segment_ids, routes, cotangent, attn_gain, query_weight, key_weight, value_weight,
    output_weight, expert_gain, router_weight, expert_in, expert_out,
):
    V, A, S = spec_vmem(), spec_any(), spec_smem()
    iz, ih, ix, ic, il = [lax.axis_index(name) for name in AX]
    where = jnp.stack([iz, ih, ix, ic, il]).astype(jnp.int32)
    cos_np, sin_np = rope_tables()
    cos_full, sin_full = jnp.asarray(cos_np), jnp.asarray(sin_np)

    ints = jnp.concatenate(
        [routes.reshape(TOK, TOPK).T, segment_ids.reshape(1, TOK), jnp.zeros((7, TOK), jnp.int32)], axis=0
    ).astype(bf16)
    ints = jnp.pad(ints, ((0, 0), (0, D - TOK)))
    x_one = jnp.concatenate([tokens.reshape(TOK, D), ints], axis=0)
    g_own = jnp.concatenate([cotangent.reshape(TOK, D), ints], axis=0)
    small = jnp.concatenate(
        [router_weight, attn_gain[:, None], expert_gain[:, None], jnp.zeros((12, 46), bf16)], axis=1
    )
    heads = jnp.concatenate(
        [
            query_weight.reshape(12, 8, 192),
            key_weight.reshape(12, 8, 64),
            value_weight.reshape(12, 8, 64),
            jnp.broadcast_to(small[:, None, :], (12, 8, 64)),
        ],
        axis=2,
    ).transpose(1, 0, 2)
    heads = jnp.broadcast_to(heads[:, None], (8, 2, 12, QKVM)).reshape(16, 12, QKVM)
    heads = lax.all_to_all(heads, ("z", "c", "yl"), split_axis=0, concat_axis=0, tiled=True)
    heads = heads.reshape(4, 48, QKVM)
    o_in = jnp.stack(
        [output_weight, send(output_weight, dl=1), send(output_weight, dc=1), send(output_weight, dc=1, dl=1)]
    )
    o48 = jnp.take(o_in, (ic * 2 + il) ^ jnp.arange(4), axis=0, mode="clip").reshape(48, D)
    heads, o48, expert_in, x_first = lax.optimization_barrier((heads, o48, expert_in, x_one))
    x_own = jnp.stack([x_first] + [send(x_first, dz=j) for j in (1, 2, 3)])
    o48 = jnp.pad(o48.reshape(48, 6, 256), ((0, 0), (0, 2), (0, 0))).transpose(1, 0, 2)
    both = jnp.concatenate([heads, o48[:4], o48[4:]], axis=2)
    other = send(both, dh=1, dl=1)
    e_out = expert_out.reshape(8, 8, 3, 512).transpose(0, 2, 1, 3).reshape(8, 24, 512)
    e_pack = jnp.concatenate([expert_in, e_out], axis=2)
    e_pack = lax.all_to_all(e_pack, ("x", "c"), split_axis=0, concat_axis=0, tiled=True)
    g_y = jnp.stack([g_own, send(g_own, dl=1)])
    other, e_pack, x_own, g_y = lax.optimization_barrier((other, e_pack, x_own, g_y))
    o_mine = jnp.where(ih == ic, both[:, :, QKVM:], other[:, :, QKVM:])
    both = jnp.stack(
        [
            jnp.concatenate([both[:, :, :QKVM], o_mine[:, :, :256]], axis=2),
            jnp.concatenate([other[:, :, :QKVM], o_mine[:, :, 256:]], axis=2),
        ]
    )
    w_pieces = [both] + [send(both, dx=k) for k in (1, 2, 3)]
    dense = [(p, A) for p in w_pieces]
    x_sib = send(x_own, dc=1)
    x_all = [(x_own, V), (x_sib, V)]

    g_y, _ = lax.optimization_barrier((g_y, w_pieces))
    g_xy = [g_y] + [send(g_y, dx=k) for k in (1, 2, 3)]

    e_out = e_pack[:, :, 1024:].reshape(8, 3, 8, 512).transpose(1, 0, 2, 3).reshape(192, 512)
    e_pack = jnp.concatenate([e_pack[:, :, :1024].reshape(192, 1024), e_out], axis=1)
    e_full = lax.all_gather(e_pack, ("z", "yh"), axis=0, tiled=True)

    normed, qk_b, v_b, mixed, misc, part_own, part_sib = call(
        kernel_attn,
        [
            ((ROWS, D), bf16, V), ((ROWS, QK), bf16, V), ((ROWS, 128), bf16, V), ((ROWS, HQ), bf16, V),
            ((64, D), bf16, V), ((4, TOK, D), f32, V), ((4, TOK, D), bf16, V),
        ],
        [(where, S), (cos_full, V), (sin_full, V)] + x_all + dense,
        [
            pltpu.VMEM((D, QKVM), bf16), pltpu.VMEM((HQ, D), bf16),
            pltpu.SemaphoreType.DMA((32,)), pltpu.SemaphoreType.DMA((24,)),
        ],
        flops=2 * ROWS * D * 512, nbytes=12 * 2**20, name="attention",
    )

    def core_sum(own, sib):
        return call(
            kernel_core_sum, [((TOK, D), bf16, V)] * 4, [(own, V), (send(sib, dc=1), V)],
            flops=10**6, nbytes=6 * 2**20, name="core_sum",
        )

    def team_sum(parts):
        return [parts[0]] + [send(parts[j], dz=j) for j in (1, 2, 3)]

    (attn_parts,) = call(
        kernel_core_sum_z, [((4, TOK, D), bf16, V)], [(where, S), (part_own, V), (send(part_sib, dc=1), V)],
        flops=10**6, nbytes=6 * 2**20, name="core_sum",
    )
    attn_parts = lax.all_to_all(attn_parts, "z", split_axis=0, concat_axis=0, tiled=True)
    resid, n2, gates, n2_a, n2_b = call(
        kernel_resid,
        [
            ((TOK, D), f32, V), ((TOK, D), bf16, V), ((16, TOK), f32, V),
            ((8, SEQ, D), bf16, V), ((8, SEQ, D), bf16, V),
        ],
        [(x_one, V), (attn_parts, V), (misc, V)],
        flops=10**7, nbytes=6 * 2**20, name="residual_norm",
    )

    def group_exchange(value):
        return lax.all_to_all(value, ("x", "yl"), split_axis=0, concat_axis=0, tiled=True)

    dn, mix, kept = [], [], []
    n2_a, g_xy = lax.optimization_barrier((n2_a, g_xy))
    g_all = g_xy + [send(item, dc=1) for item in g_xy]
    group_rows = [group_exchange(n2_a), group_exchange(n2_b)]
    group_rows[0], g_all = lax.optimization_barrier((group_rows[0], g_all))
    for half, rows in enumerate(group_rows):
        if half:
            rows, _ = lax.optimization_barrier((rows, outs[0]))
        rows_sib = send(rows, dc=1)
        outs = call(
            functools.partial(kernel_expert, half),
            [
                ((8, 80, D), bf16, A), ((8, SEQ, D), bf16, A),
                ((512, D), bf16, A), ((512, D), bf16, A), ((512, F), bf16, A), ((512, 1024), bf16, A),
            ]
            + [((2, 80, D), bf16, A)] * 4
            + [((8, SEQ, D), bf16, A)],
            [(where, S), (misc, V), (rows, A), (rows_sib, A), (e_full, A)] + [(p, A) for p in g_all],
            [
                pltpu.VMEM((16, SEQ, D), bf16), pltpu.VMEM((16, 80, D), bf16),
                pltpu.VMEM((D, 1024), bf16), pltpu.VMEM((F, D), bf16),
                pltpu.VMEM((16, SEQ), f32), pltpu.VMEM((16, SEQ), f32), pltpu.VMEM((16, 1024), f32),
                pltpu.VMEM((512, D), bf16), pltpu.VMEM((512, D), bf16), pltpu.VMEM((512, F), bf16),
                pltpu.VMEM((512, 1024), bf16), pltpu.VMEM((16, 80, D), bf16), pltpu.VMEM((16, SEQ, D), bf16),
                pltpu.SemaphoreType.DMA((2,)), pltpu.SemaphoreType.DMA((32,)), pltpu.SemaphoreType.DMA((32,)),
                pltpu.SemaphoreType.DMA((18,)),
            ],
            flops=6 * 10**9, nbytes=30 * 2**20, name="experts",
        )
        recv = [send(v, dc=1) for v in outs[6:10]]
        if half:
            recv, dn[0] = lax.optimization_barrier((recv, dn[0]))
        (summed,) = call(
            kernel_pair_sum, [((8, 80, D), bf16, V)], [(outs[0], V)] + [(v, V) for v in recv],
            flops=10**7, nbytes=6 * 2**20, name="pair_sum",
        )
        dn.append(group_exchange(summed))
        mix.append((outs[1], outs[10]))
        kept.extend(outs[2:6])
    kept[0], _ = lax.optimization_barrier((kept[0], summed))
    (e_grad,) = call(
        kernel_expert_grads, [((D, D), bf16, V)], [(v, V) for v in kept],
        flops=6 * 10**9, nbytes=14 * 2**20, name="expert_gradients",
    )
    mix[1], _ = lax.optimization_barrier((mix[1], e_grad))
    mix_in = [(v, V) for own, sib in mix for v in (own, send(sib, dc=1))]
    mix_sum = call(
        kernel_mix_sum, [((2, SEQ, D), bf16, V)] * 8, [(where, S)] + mix_in,
        flops=10**7, nbytes=10 * 2**20, name="mix_sum",
    )
    dn[1], e_grad, mix_sum = lax.optimization_barrier((dn[1], e_grad, mix_sum))
    dresid, dattn, small_grad = call(
        kernel_home,
        [((TOK, D), f32, V), ((4, TOK, D), bf16, V), ((32, D), f32, V)],
        [(g_own, V), (resid, V), (n2, V), (gates, V), (misc, V), (dn[0], V), (dn[1], V)],
        [pltpu.VMEM((16, TOK), f32)],
        flops=10**8, nbytes=6 * 2**20, name="home_gradient",
    )
    e_grad, dattn = lax.optimization_barrier((e_grad, dattn))
    e_sum = lax.psum_scatter(e_grad, ("z", "yh"), scatter_dimension=0, tiled=True)
    da_own = lax.all_to_all(dattn, "z", split_axis=0, concat_axis=0, tiled=True)
    mix_x = [[mix_sum[h4]] + [send(mix_sum[h4 + k], dx=k) for k in (1, 2, 3)] for h4 in (0, 4)]
    da_own, mix_x[0] = lax.optimization_barrier((da_own, mix_x[0]))
    da_all = [da_own, send(da_own, dc=1)]
    wg_out, dcat = call(
        kernel_back,
        [((4, 2, 4, 48, WIDE), bf16, A), ((ROWS, QKVM), bf16, V)],
        [
            (where, S), (normed, V), (qk_b, V), (v_b, V), (mixed, V), (small_grad, V), (cos_full, V), (sin_full, V),
            (x_own, A), (x_sib, A),
        ]
        + [(p, V) for p in da_all]
        + dense,
        [
            pltpu.VMEM((D, QKVM), bf16), pltpu.VMEM((HQ, D), bf16), pltpu.VMEM((ROWS, D), bf16),
            pltpu.VMEM((ROWS, HQ), bf16), pltpu.VMEM((ROWS, QK), f32),
            pltpu.VMEM((D, QKVM), bf16), pltpu.VMEM((HQ, D + 512), bf16), pltpu.VMEM((8, 16, TOK), bf16),
            pltpu.SemaphoreType.DMA((32,)), pltpu.SemaphoreType.DMA((24,)), pltpu.SemaphoreType.DMA((64,)),
            pltpu.SemaphoreType.DMA((8,)),
        ],
        flops=6 * ROWS * D * 512, nbytes=20 * 2**20, name="attention_back",
    )
    wg_out, mix_x[1] = lax.optimization_barrier((wg_out, mix_x[1]))
    wg = lax.all_to_all(wg_out, "x", split_axis=0, concat_axis=0, tiled=True)
    mix_keep, mix_give = call(
        kernel_mix_pair, [((TOK, D), bf16, V)] * 2, [(where, S)] + [(p, V) for p in mix_x[0] + mix_x[1]],
        flops=10**6, nbytes=5 * 2**20, name="mix_pair",
    )
    dn1_own, dn1_sib = call(
        kernel_back_tokens,
        [((4, TOK, D), f32, V), ((4, TOK, D), bf16, V)],
        [(where, S), (dcat, V)] + dense,
        [pltpu.VMEM((D, QKVM), bf16), pltpu.SemaphoreType.DMA((32,))],
        flops=2 * ROWS * D * QKVM, nbytes=10 * 2**20, name="token_back",
    )
    wg, dn1_own, dn1_sib, mix_keep, mix_give = lax.optimization_barrier((wg, dn1_own, dn1_sib, mix_keep, mix_give))
    dn1_parts = core_sum(dn1_own, dn1_sib)
    (block_out,) = call(
        kernel_block_out, [((TOK, D), bf16, V)],
        [(g_own, V), (resid, V), (mix_keep, V), (send(mix_give, dl=1), V)],
        flops=10**7, nbytes=5 * 2**20, name="block_output",
    )
    dn1_pieces = team_sum(dn1_parts)
    keep, give = call(
        kernel_dense_sum, [((4, 48, QKVM + 384), bf16, V)] * 2, [(where, S), (wg, V)],
        flops=10**6, nbytes=5 * 2**20, name="dense_sum",
    )
    take = send(give, dh=1, dl=1)
    e_sum, _ = lax.optimization_barrier((e_sum, give))
    ge_out = e_sum[:, 1024:].reshape(3, 8, 8, 512).transpose(1, 0, 2, 3).reshape(8, 24, 512)
    ge = jnp.concatenate([e_sum[:, :1024].reshape(8, 24, 1024), ge_out], axis=2)
    ge = lax.all_to_all(ge, ("x", "c"), split_axis=0, concat_axis=0, tiled=True)
    keep = (keep.astype(f32) + take.astype(f32)).astype(bf16)
    keep, ge = lax.optimization_barrier((keep, ge))
    heads = keep[:, :, :QKVM].reshape(16, 12, QKVM)
    heads = lax.all_to_all(heads, ("z", "c", "yl"), split_axis=0, concat_axis=0, tiled=True)
    heads, dn1_pieces, keep = lax.optimization_barrier((heads, dn1_pieces, keep))
    (token_grad,) = call(
        kernel_token_grad, [((TOK, D), bf16, V)],
        [(x_one, V), (dresid, V)] + [(p, V) for p in dn1_pieces] + [(misc, V)],
        flops=10**7, nbytes=3 * 2**20, name="token_gradient",
    )
    back = keep[:, :, QKVM:].transpose(1, 0, 2).reshape(4, 12, D)
    me = ic * 2 + il
    d_o = pick(back, 0, me).astype(f32) + send(pick(back, 0, me ^ 1), dl=1).astype(f32)
    d_o = d_o + send(pick(back, 0, me ^ 2), dc=1).astype(f32) + send(pick(back, 0, me ^ 3), dc=1, dl=1).astype(f32)
    ge = ge.astype(f32)
    ge_in = ge[:, :, :1024]
    ge_out = ge[:, :, 1024:].reshape(8, 3, 8, 512).transpose(0, 2, 1, 3).reshape(8, 8, D)
    heads = heads.astype(f32).reshape(8, 2, 12, QKVM).sum(axis=1)
    dq = heads[:, :, :HQ].transpose(1, 0, 2).reshape(12, D)
    dk = heads[:, :, HQ:QK].transpose(1, 0, 2).reshape(12, 512)
    dv = heads[:, :, QK:QKV].transpose(1, 0, 2).reshape(12, 512)
    d_small = heads[:, :, QKV:].sum(axis=0)
    return (
        block_out.reshape(2, SEQ, D),
        token_grad.reshape(2, SEQ, D),
        d_small[:, 16],
        dq,
        dk,
        dv,
        d_o,
        d_small[:, 17],
        d_small[:, :16],
        ge_in,
        ge_out,
    )


def solution(mesh):
    devices = mesh.devices.reshape(DIMS) if hasattr(mesh, "devices") else None
    fine = Mesh(devices, AX)
    every = ("z", "yh", "x", "c", "yl")
    dp = ("z", "yh", "x", "c")
    in_specs = (
        P(every, None, None), P(every, None), P(every, None, None), P(every, None, None), P(every),
        P(every, None), P(every, None), P(every, None), P(every, None), P(every), P(every, None),
        P("yl", dp, None), P("yl", dp, None),
    )
    out_specs = (
        P(every, None, None), P(every, None, None), P(every), P(every, None), P(every, None),
        P(every, None), P(every, None), P(every), P(every, None), P("yl", dp, None), P("yl", dp, None),
    )
    return jax.shard_map(on_device, mesh=fine, in_specs=in_specs, out_specs=out_specs, check_vma=False)
```

```python
import functools

import jax
import jax.numpy as jnp
import numpy as np
from jax import lax
from jax.experimental import pallas as pl
from jax.experimental.pallas import tpu as pltpu
from jax.sharding import Mesh
from jax.sharding import PartitionSpec as P

D = 1536
Q_HEADS = 24
KV_HEADS = 8
HEAD_DIM = 64
F = 512
TOPK = 8
EXPERTS = 16
SEQ = 64
CAP = 32

AX = ("z", "yh", "x", "c", "yl")
DIMS = (4, 2, 4, 2, 2)
EPS = 1e-5
NEG = -1e30
TOK = 128
EXT = 144
HQ = 192
QK = 256
QKV = 320
QKVM = 384
WIDE = 640
ROWS = 1024
bf16 = jnp.bfloat16
f32 = jnp.float32


def coords_list():
    return list(np.ndindex(*DIMS))


def send(value, dz=0, dh=0, dx=0, dc=0, dl=0):
    flat = {pos: i for i, pos in enumerate(coords_list())}
    pairs = [
        (i, flat[(z ^ dz, h ^ dh, x ^ dx, c ^ dc, l ^ dl)])
        for (z, h, x, c, l), i in flat.items()
    ]
    return lax.ppermute(value, AX, pairs)


def dot(a, b):
    return jnp.dot(a, b, preferred_element_type=f32)


def dot_t(a, b):
    return lax.dot_general(a, b, (((1,), (1,)), ((), ())), preferred_element_type=f32)


def t_dot(a, b):
    return lax.dot_general(a, b, (((0,), (0,)), ((), ())), preferred_element_type=f32)


def params(mib=60):
    return pltpu.CompilerParams(vmem_limit_bytes=mib * 2**20)


def rope_tables():
    angle = np.arange(SEQ)[:, None] * (10000.0 ** (-np.arange(32) * 2.0 / 64))[None, :]
    cosine, sine = np.cos(angle), np.sin(angle)
    cos_full = np.concatenate([cosine, cosine] * 2, axis=1)
    sin_full = np.concatenate([-sine, sine] * 2, axis=1)
    return np.tile(cos_full, (4, 1)).astype(np.float32), np.tile(sin_full, (4, 1)).astype(np.float32)


def turn(values, cos_full, sin_full):
    width = values.shape[1]
    lane = lax.broadcasted_iota(jnp.int32, values.shape, 1)
    ahead = pltpu.roll(values, width - 32, 1)
    behind = pltpu.roll(values, 32, 1)
    partner = jnp.where((lane % 64) < 32, ahead, behind)
    copies = width // 128
    cos_wide = jnp.concatenate([cos_full] * copies, axis=1)
    sin_wide = jnp.concatenate([sin_full] * copies, axis=1)
    return values * cos_wide + partner * sin_wide


def allowed_mask(ints):
    row = jnp.broadcast_to(ints[8:9, :], (TOK, TOK))
    col = row.T
    p = lax.broadcasted_iota(jnp.int32, (TOK, TOK), 0)
    t = lax.broadcasted_iota(jnp.int32, (TOK, TOK), 1)
    return (row == col) & (t <= p) & ((p < SEQ) == (t < SEQ))


def qkv_copies(pieces, target, sems, h, x):
    copies = []
    for k in range(4):
        for b in range(2):
            for zz in range(4):
                start = pl.multiple_of(((zz * 2 + (h ^ b)) * 4 + (x ^ k)) * 48, 16)
                copies.append(
                    pltpu.make_async_copy(
                        pieces[k].at[b, zz, :, pl.ds(0, QKVM)],
                        target.at[pl.ds(start, 48), :],
                        sems.at[(k * 2 + b) * 4 + zz],
                    )
                )
    return copies


def o_copies(pieces, target, sems, x):
    copies = []
    for k in range(4):
        for q in range(6):
            start = pl.multiple_of((x ^ k) * 48, 16)
            copies.append(
                pltpu.make_async_copy(
                    pieces[k].at[q // 4, q % 4, :, pl.ds(QKVM, 256)],
                    target.at[pl.ds(start, 48), pl.ds(256 * q, 256)],
                    sems.at[k * 6 + q],
                )
            )
    return copies


def spec_any():
    return pl.BlockSpec(memory_space=pl.ANY)


def spec_vmem():
    return pl.BlockSpec(memory_space=pltpu.VMEM)


def spec_smem():
    return pl.BlockSpec(memory_space=pltpu.SMEM)


def unit(size):
    row = lax.broadcasted_iota(jnp.int32, (size, size), 0)
    return (row == lax.broadcasted_iota(jnp.int32, (size, size), 1)).astype(f32).astype(bf16)


def kernel_attn(where, cos_ref, sin_ref, x_own, x_sib, *rest):
    x_in = [x_own.at[j] for j in range(4)] + [x_sib.at[j] for j in range(4)]
    w_in = rest[:4]
    normed_out, qk_ref, v_ref, mixed_ref, misc_ref, own_out, sib_out = rest[4:11]
    w, wo, normed_ref, own_ref, sib_ref, sems, osems, out_sem = rest[11:]
    going = []

    def give(src, dst):
        copy = pltpu.make_async_copy(src, dst, out_sem.at[len(going)])
        copy.start()
        going.append(copy)

    copies = qkv_copies(w_in, w, sems, where[1], where[2])
    more = o_copies(w_in, wo, osems, where[2])
    for item in copies + more:
        item.start()
    for item in copies:
        item.wait()
    misc = dot_t(unit(64), w[:, QKV:])
    misc_ref[...] = misc.astype(bf16)
    gain = misc[16:17, :]
    for m in range(8):
        rows = slice(m * TOK, (m + 1) * TOK)
        xin = x_in[m][0:TOK, :].astype(f32)
        rinv = lax.rsqrt(jnp.mean(xin * xin, axis=1, keepdims=True) + EPS)
        normed_ref[rows, :] = (xin * rinv * gain).astype(bf16)
    give(normed_ref, normed_out)
    cos_full, sin_full = cos_ref[...], sin_ref[...]
    for m in range(4):
        rows = slice(m * 256, (m + 1) * 256)
        qkv = dot(normed_ref[rows, :], w[:, 0:QKVM])
        qk_ref[rows, :] = turn(qkv[:, 0:QK], cos_full, sin_full).astype(bf16)
        v_ref[rows, :] = qkv[:, QK:QKVM].astype(bf16)
    for m in range(8):
        ok = allowed_mask(x_in[m][TOK:EXT, :TOK].astype(f32))
        ok3 = jnp.concatenate([ok.astype(f32)] * 3, axis=0) > 0.5
        rows = slice(m * TOK, (m + 1) * TOK)
        keys = qk_ref[rows, HQ:QK]
        vals = v_ref[rows, 0:64]
        q3 = jnp.concatenate([qk_ref[rows, g * 64 : (g + 1) * 64] for g in range(3)], axis=0)
        scores = jnp.where(ok3, dot_t(q3, keys) * 0.125, NEG)
        top = jnp.max(scores, axis=1, keepdims=True)
        expo = jnp.exp(scores - top)
        probs = (expo / jnp.sum(expo, axis=1, keepdims=True)).astype(bf16)
        out = dot(probs, vals).astype(bf16)
        for g in range(3):
            mixed_ref[rows, g * 64 : (g + 1) * 64] = out[g * TOK : (g + 1) * TOK, :]
    for item in more:
        item.wait()
    for m in range(4):
        rows = slice((4 + m) * TOK, (5 + m) * TOK)
        sib_ref[m] = dot(mixed_ref[rows, :], wo[...]).astype(bf16)
        give(sib_ref.at[m], sib_out.at[m])
    for m in range(4):
        rows = slice(m * TOK, (m + 1) * TOK)
        own_ref[m] = dot(mixed_ref[rows, :], wo[...])
        give(own_ref.at[m], own_out.at[m])
    for copy in going:
        copy.wait()


def kernel_core_sum(own_ref, recv_ref, *outs):
    for m in range(4):
        outs[m][...] = (own_ref[m] + recv_ref[m].astype(f32)).astype(bf16)


def kernel_core_sum_z(where, own_ref, recv_ref, out_ref):
    for m in range(4):
        out_ref[where[0] ^ m] = (own_ref[m] + recv_ref[m].astype(f32)).astype(bf16)


def chosen_gates(misc, n2, ints):
    logits = dot_t(misc, n2)
    expert = lax.broadcasted_iota(jnp.int32, logits.shape, 0).astype(f32)
    hot = jnp.zeros(logits.shape, f32)
    for k in range(TOPK):
        hot = jnp.maximum(hot, (expert == ints[k : k + 1, :]).astype(f32))
    masked = jnp.where(hot > 0.5, logits, NEG)
    expo = jnp.where(hot > 0.5, jnp.exp(masked - jnp.max(masked, axis=0, keepdims=True)), 0.0)
    return expo / jnp.sum(expo, axis=0, keepdims=True)


def kernel_resid(xo, parts, misc_ref, resid_ref, n2_ref, gates_ref, na_ref, nb_ref):
    resid = xo[:TOK, :].astype(f32)
    for m in range(4):
        resid = resid + parts[m].astype(f32)
    resid_ref[...] = resid
    rinv = lax.rsqrt(jnp.mean(resid * resid, axis=1, keepdims=True) + EPS)
    n2 = (resid * rinv * misc_ref[17:18, :].astype(f32)).astype(bf16)
    n2_ref[...] = n2
    for m in range(8):
        na_ref[m] = n2[:SEQ, :]
        nb_ref[m] = n2[SEQ:, :]
    gates_ref[...] = chosen_gates(misc_ref[0:16, :], n2, xo[TOK:EXT, :TOK].astype(f32))


def kernel_expert(half, where, misc_ref, n2_own, n2_sib, w_ref, *rest):
    gx_in = rest[:8]
    dn_own, mix_own, disp_out, dslot_out, hid_out, dgu_out = rest[8:14]
    dn_sib, mix_sib = rest[14:18], rest[18]
    (n2, gx, win, wout, slot_s, gate_s, ints_s, disp, dslot, hid, dgu, dn_s, mix_s,
     n2_sem, gx_sem, w_sem, out_sem) = rest[19:]
    x, c, l = where[2], where[3], where[4]
    me = (l * 8 + x * 2 + c).astype(f32)
    w_copies = []
    for blk in range(8):
        w_copies.append(
            pltpu.make_async_copy(
                w_ref.at[pl.ds(blk * 192, 192), pl.ds(0, 1024)], win.at[pl.ds(blk * 192, 192), :], w_sem.at[blk * 4]
            )
        )
        for t in range(3):
            w_copies.append(
                pltpu.make_async_copy(
                    w_ref.at[pl.ds(blk * 192 + 64 * t, 64), pl.ds(1024, 512)],
                    wout.at[pl.ds(blk * 64, 64), pl.ds(512 * t, 512)],
                    w_sem.at[blk * 4 + 1 + t],
                )
            )
    n2_copies = [
        pltpu.make_async_copy(n2_own, n2.at[pl.ds(0, 8)], n2_sem.at[0]),
        pltpu.make_async_copy(n2_sib, n2.at[pl.ds(8, 8)], n2_sem.at[1]),
    ]
    gx_copies = []
    for core in range(2):
        for k in range(4):
            for b in range(2):
                at = core * 8 + (x ^ k) * 2 + (l ^ b)
                g_src = gx_in[core * 4 + k].at[b]
                gx_copies.append(
                    pltpu.make_async_copy(
                        g_src.at[pl.ds(SEQ * half, SEQ), :], gx.at[at, pl.ds(0, SEQ), :], gx_sem.at[(core * 8 + k * 2 + b) * 2]
                    )
                )
                gx_copies.append(
                    pltpu.make_async_copy(
                        g_src.at[pl.ds(TOK, 16), :], gx.at[at, pl.ds(SEQ, 16), :], gx_sem.at[(core * 8 + k * 2 + b) * 2 + 1]
                    )
                )
    for item in gx_copies + n2_copies + w_copies:
        item.start()
    for item in gx_copies + n2_copies:
        item.wait()
    for m in range(16):
        ints_s[:, SEQ * m : SEQ * (m + 1)] = gx[m, SEQ : SEQ + 16, SEQ * half : SEQ * (half + 1)].astype(f32)
    token = lax.broadcasted_iota(jnp.int32, (TOK, TOK), 0)
    after = lax.broadcasted_iota(jnp.int32, (TOK, TOK), 1)
    before = ((token < after) & ((token < SEQ) == (after < SEQ))).astype(f32).astype(bf16)
    for core in range(2):
        lanes = slice(core * 512, core * 512 + 512)
        ints = ints_s[:, lanes]
        gates = chosen_gates(misc_ref[0:16, :], n2[8 * core : 8 * core + 8].reshape(512, D), ints)
        expert = lax.broadcasted_iota(jnp.int32, gates.shape, 0).astype(f32)
        gate = jnp.sum(jnp.where(expert == me, gates, 0.0), axis=0, keepdims=True)
        hit = jnp.max((ints[0:8, :] == me).astype(f32), axis=0, keepdims=True)
        hit = hit * (ints[8:9, :] > 0.5).astype(f32)
        rank = jnp.concatenate(
            [
                dot(jnp.broadcast_to(hit[:, u * TOK : (u + 1) * TOK], (16, TOK)).astype(bf16), before)[0:1, :]
                for u in range(4)
            ],
            axis=1,
        )
        slot = jnp.where((hit > 0.5) & (rank < CAP - 0.5), rank, -1.0)
        for q in range(8):
            slot_s[core * 8 + q : core * 8 + q + 1, :] = slot[:, q * SEQ : (q + 1) * SEQ]
            gate_s[core * 8 + q : core * 8 + q + 1, :] = gate[:, q * SEQ : (q + 1) * SEQ]
    slot_iota = lax.broadcasted_iota(jnp.int32, (CAP, SEQ), 0).astype(f32)
    line = lax.broadcasted_iota(jnp.int32, (16, SEQ), 0)
    going = []

    def give(src, dst):
        copy = pltpu.make_async_copy(src, dst, out_sem.at[len(going)])
        copy.start()
        going.append(copy)

    for i in range(2):
        rows = slice(i * 256, (i + 1) * 256)
        hots, gate_cols, g_parts = [], [], []
        for q in range(8):
            m = i * 8 + q
            hot = (slot_iota == slot_s[m : m + 1, :]).astype(f32)
            gate_col = jnp.sum(hot * gate_s[m : m + 1, :], axis=1, keepdims=True)
            hot_b = hot.astype(bf16)
            hots.append(hot_b)
            gate_cols.append(gate_col)
            srows = slice(i * 256 + q * CAP, i * 256 + (q + 1) * CAP)
            disp[srows, :] = dot(hot_b, n2[m]).astype(bf16)
            gsl = dot(hot_b, gx[m, 0:SEQ, :])
            g_parts.append(gsl)
            dslot[srows, :] = (gate_col * gsl).astype(bf16)
        give(disp.at[rows, :], disp_out.at[rows, :])
        give(dslot.at[rows, :], dslot_out.at[rows, :])
        if i == 0:
            for item in w_copies:
                item.wait()
        gup = dot(disp[rows, :], win[...])
        gate_part, up_part = gup[:, :F], gup[:, F:]
        sig = jax.nn.sigmoid(gate_part)
        hidden = (gate_part * sig * up_part).astype(bf16)
        hid[rows, :] = hidden
        give(hid.at[rows, :], hid_out.at[rows, :])
        dhid = dot_t(dslot[rows, :], wout[...])
        silu_grad = sig * (1.0 + gate_part * (1.0 - sig))
        dg = jnp.concatenate([dhid * up_part * silu_grad, dhid * gate_part * sig], axis=1).astype(bf16)
        dgu[rows, :] = dg
        give(dgu.at[rows, :], dgu_out.at[rows, :])
        out_rows = dot(hidden, wout[...]).astype(bf16).astype(f32)
        for q in range(8):
            part = slice(q * CAP, (q + 1) * CAP)
            m = i * 8 + q
            dgate = jnp.sum(g_parts[q] * out_rows[part, :], axis=1, keepdims=True)
            dgate_row = jnp.sum(hots[q].astype(f32) * dgate, axis=0, keepdims=True)
            high = dgate_row.astype(bf16).astype(f32)
            low = dgate_row - high
            extra = jnp.where(line == 2 * c, high, 0.0) + jnp.where(line == 2 * c + 1, low, 0.0)
            dn_s[m, SEQ : SEQ + 16, :] = jnp.zeros((16, D), bf16)
            dn_s[m, SEQ : SEQ + 16, 0:SEQ] = extra.astype(bf16)
            weighted = (gate_cols[q] * out_rows[part, :]).astype(bf16)
            mix_s[m, :, :] = t_dot(hots[q], weighted).astype(bf16)
        if i == 0:
            give(mix_s.at[pl.ds(0, 8)], mix_own)
        else:
            give(mix_s.at[pl.ds(8, 8)], mix_sib)
        din = dot_t(dg, win[...]).astype(bf16)
        for q in range(8):
            dn_s[i * 8 + q, 0:SEQ, :] = t_dot(hots[q], din[q * CAP : (q + 1) * CAP, :]).astype(bf16)
        if i == 0:
            give(dn_s.at[pl.ds(0, 8)], dn_own)
        else:
            for k in range(4):
                give(dn_s.at[pl.ds(8 + 2 * k, 2)], dn_sib[k])
    for copy in going:
        copy.wait()


def kernel_expert_grads(disp_a, dslot_a, hid_a, dgu_a, disp_b, dslot_b, hid_b, dgu_b, wg):
    for n in range(6):
        cols = slice(n * 256, (n + 1) * 256)
        wg[cols, 0:1024] = (t_dot(disp_a[:, cols], dgu_a[...]) + t_dot(disp_b[:, cols], dgu_b[...])).astype(bf16)
    for n in range(2):
        cols = slice(n * 256, (n + 1) * 256)
        out_g = (t_dot(hid_a[:, cols], dslot_a[...]) + t_dot(hid_b[:, cols], dslot_b[...])).astype(bf16)
        for b in range(4):
            blk = n * 4 + b
            for t in range(3):
                wg[blk * 192 + t * 64 : blk * 192 + (t + 1) * 64, 1024:1536] = out_g[
                    b * 64 : (b + 1) * 64, t * 512 : (t + 1) * 512
                ]


def kernel_pair_sum(*refs):
    out = refs[-1]
    lines = 0
    for i in range(0, len(refs) - 1, 5):
        size = refs[i].shape[1]
        for m in range(8):
            total = refs[i][m].astype(f32) + refs[i + 1 + m // 2][m % 2].astype(f32)
            out[m, lines : lines + size, :] = total.astype(bf16)
        lines += size


def kernel_mix_sum(where, own_a, sib_a, own_b, sib_b, *outs):
    for half, (own, sib) in enumerate(((own_a, sib_a), (own_b, sib_b))):
        for k in range(4):
            for ll in range(2):
                m = (where[2] ^ k) * 2 + ll
                outs[half * 4 + k][ll] = (own[m].astype(f32) + sib[m].astype(f32)).astype(bf16)


def kernel_mix_pair(where, *refs):
    l = where[4]
    for out, line in ((refs[8], l), (refs[9], 1 - l)):
        for half in range(2):
            total = refs[half * 4][line].astype(f32)
            for k in range(1, 4):
                total = total + refs[half * 4 + k][line].astype(f32)
            out[SEQ * half : SEQ * (half + 1), :] = total.astype(bf16)


def kernel_home(gx_ref, resid_ref, n2_ref, gates_ref, misc_ref, dn_a, dn_b, dresid_ref, dattn_ref, small_ref, dg_s):
    for xx in range(4):
        for ll in range(2):
            for half, dn in enumerate((dn_a, dn_b)):
                extra = dn[xx * 2 + ll, SEQ : SEQ + 16, 0:SEQ].astype(f32)
                first = ll * 8 + xx * 2
                lanes = slice(SEQ * half, SEQ * (half + 1))
                dg_s[first : first + 1, lanes] = extra[0:1, :] + extra[1:2, :]
                dg_s[first + 1 : first + 2, lanes] = extra[2:3, :] + extra[3:4, :]
    gates = gates_ref[...]
    dgates = dg_s[...]
    dlog = (gates * (dgates - jnp.sum(gates * dgates, axis=0, keepdims=True))).astype(bf16)
    valid_row = jnp.broadcast_to((gx_ref[TOK + 8 : TOK + 9, :TOK].astype(f32) > 0.5).astype(f32), (TOK, TOK))
    valid = valid_row.T[:, 0:1]
    total = t_dot(dlog, misc_ref[0:16, :])
    sums = []
    for dn in (dn_a, dn_b):
        part = dn[0, 0:SEQ, :].astype(f32)
        for m in range(1, 8):
            part = part + dn[m, 0:SEQ, :].astype(f32)
        sums.append(part)
    total = total + jnp.concatenate(sums, axis=0)
    resid = resid_ref[...]
    rinv = lax.rsqrt(jnp.mean(resid * resid, axis=1, keepdims=True) + EPS)
    u = total * misc_ref[17:18, :].astype(f32)
    g = gx_ref[0:TOK, :].astype(f32) * valid
    dresid = g + rinv * u - resid * (rinv * rinv * rinv) * jnp.mean(u * resid, axis=1, keepdims=True)
    dresid_ref[...] = dresid
    for m in range(4):
        dattn_ref[m] = dresid.astype(bf16)
    small_ref[0:16, :] = dot(dlog, n2_ref[...])
    gain = jnp.sum(total * resid * rinv, axis=0, keepdims=True)
    line = lax.broadcasted_iota(jnp.int32, (16, D), 0)
    small_ref[16:32, :] = jnp.where(line == 1, gain, 0.0)


def kernel_back(
    where, normed_ref, qk_ref, v_ref, mixed_ref, small_ref, cos_ref, sin_ref, x_own, x_sib, da_own, da_sib, *rest
):
    da_in = [da_own.at[where[0] ^ j] for j in range(4)] + [da_sib.at[where[0] ^ j] for j in range(4)]
    w_in = rest[:4]
    w_out, dcat = rest[4:6]
    w, wo, da, dmixed, dqk, wg, og, ints, normed, sems, osems, gsems, isems = rest[6:]
    h, x = where[1], where[2]
    o_in = o_copies(w_in, wo, osems, x)
    copies = qkv_copies(w_in, w, sems, h, x)
    marks = [
        pltpu.make_async_copy(
            (x_own, x_sib)[m // 4].at[m % 4, pl.ds(TOK, 16), pl.ds(0, TOK)], ints.at[m], isems.at[m]
        )
        for m in range(8)
    ]
    rows_in = pltpu.make_async_copy(normed_ref, normed, isems.at[8])
    for item in marks + o_in + copies + [rows_in]:
        item.start()
    for m in range(8):
        da[m * TOK : (m + 1) * TOK, :] = da_in[m][...]
    for item in o_in:
        item.wait()
    for m in range(4):
        rows = slice(m * 256, (m + 1) * 256)
        dmixed[rows, :] = dot_t(da[rows, :], wo[...]).astype(bf16)
    for item in marks:
        item.wait()
    for m in range(8):
        ok = allowed_mask(ints[m].astype(f32))
        ok3 = jnp.concatenate([ok.astype(f32)] * 3, axis=0) > 0.5
        rows = slice(m * TOK, (m + 1) * TOK)
        keys = qk_ref[rows, HQ:QK]
        vals = v_ref[rows, 0:64]
        q3 = jnp.concatenate([qk_ref[rows, g * 64 : (g + 1) * 64] for g in range(3)], axis=0)
        dm3 = jnp.concatenate([dmixed[rows, g * 64 : (g + 1) * 64] for g in range(3)], axis=0)
        scores = jnp.where(ok3, dot_t(q3, keys) * 0.125, NEG)
        top = jnp.max(scores, axis=1, keepdims=True)
        expo = jnp.exp(scores - top)
        probs = expo / jnp.sum(expo, axis=1, keepdims=True)
        dprobs = dot_t(dm3, vals)
        dcat[rows, QK:QKV] = t_dot(probs.astype(bf16), dm3).astype(bf16)
        ds = (probs * (dprobs - jnp.sum(probs * dprobs, axis=1, keepdims=True))).astype(bf16)
        dq3 = dot(ds, keys) * 0.125
        for g in range(3):
            dqk[rows, g * 64 : (g + 1) * 64] = dq3[g * TOK : (g + 1) * TOK, :]
        dqk[rows, HQ:QK] = t_dot(ds, q3) * 0.125
    cos_full, sin_full = cos_ref[...], -sin_ref[...]
    for m in range(4):
        rows = slice(m * 256, (m + 1) * 256)
        dcat[rows, 0:QK] = turn(dqk[rows, :], cos_full, sin_full).astype(bf16)
    dcat[:, QKV:] = jnp.zeros((ROWS, QKVM - QKV), bf16)
    for item in copies:
        item.wait()
    og[:, 0:D] = t_dot(mixed_ref[...], da[...]).astype(bf16)
    og[:, D:] = jnp.zeros((HQ, 512), bf16)
    small = jnp.concatenate([small_ref[...], jnp.zeros((32, D), f32)], axis=0).astype(bf16)
    column = lax.broadcasted_iota(jnp.int32, (256, QKVM - QKV), 1)
    rows_in.wait()
    for n in range(6):
        rows = slice(n * 256, (n + 1) * 256)
        grad = t_dot(normed[:, rows], dcat[...])
        gain = jnp.sum(grad[:, 0:QKV] * w[rows, 0:QKV].astype(f32), axis=1, keepdims=True)
        gain = gain / w[rows, QKV + 16 : QKV + 17].astype(f32)
        wg[rows, 0:QKV] = grad[:, 0:QKV].astype(bf16)
        wg[rows, QKV:] = (t_dot(small[:, rows], unit(64)) + jnp.where(column == 16, gain, 0.0)).astype(bf16)
    outs = []
    for k in range(4):
        for b in range(2):
            for zz in range(4):
                start = pl.multiple_of(((zz * 2 + (h ^ b)) * 4 + (x ^ k)) * 48, 16)
                outs.append(
                    pltpu.make_async_copy(
                        wg.at[pl.ds(start, 48), :],
                        w_out.at[x ^ k, b, zz, :, pl.ds(0, QKVM)],
                        gsems.at[(k * 2 + b) * 4 + zz],
                    )
                )
        for q in range(8):
            start = pl.multiple_of((x ^ k) * 48, 16)
            outs.append(
                pltpu.make_async_copy(
                    og.at[pl.ds(start, 48), pl.ds(256 * q, 256)],
                    w_out.at[x ^ k, q // 4, q % 4, :, pl.ds(QKVM, 256)],
                    gsems.at[32 + k * 8 + q],
                )
            )
    for item in outs:
        item.start()
    for item in outs:
        item.wait()


def kernel_back_tokens(where, dcat_ref, *rest):
    w_in, own_ref, sib_ref, w, sems = rest[:4], rest[4], rest[5], rest[6], rest[7]
    copies = qkv_copies(w_in, w, sems, where[1], where[2])
    for item in copies:
        item.start()
    for item in copies:
        item.wait()
    w[:, QKV:] = jnp.zeros((D, QKVM - QKV), bf16)
    for m in range(4):
        own_ref[m] = dot_t(dcat_ref[m * TOK : (m + 1) * TOK, :], w[...])
        sib_ref[m] = dot_t(dcat_ref[(4 + m) * TOK : (5 + m) * TOK, :], w[...]).astype(bf16)


def kernel_dense_sum(where, *refs):
    w_in, outs = [refs[0].at[k] for k in range(4)], refs[1:3]
    here = where[1] == where[3]

    def total(b, zz, lanes):
        out = w_in[0][b, zz, :, lanes].astype(f32)
        for k in range(1, 4):
            out = out + w_in[k][b, zz, :, lanes].astype(f32)
        return out

    for b in range(2):
        for zz in range(4):
            outs[b][zz, :, 0:QKVM] = total(b, zz, slice(0, QKVM)).astype(bf16)
    for q in range(6):
        block = total(q // 4, q % 4, slice(QKVM, WIDE))
        for part in range(2):
            at = q * 2 + part
            lanes = slice(QKVM + 128 * (at % 3), QKVM + 128 * (at % 3 + 1))
            piece = block[:, 128 * part : 128 * (part + 1)]
            outs[0][at // 3, :, lanes] = jnp.where(here, piece, 0.0).astype(bf16)
            outs[1][at // 3, :, lanes] = jnp.where(here, 0.0, piece).astype(bf16)


def kernel_token_grad(xo, dresid_ref, p0, p1, p2, p3, misc_ref, out_ref):
    xin = xo[:TOK, :].astype(f32)
    rinv = lax.rsqrt(jnp.mean(xin * xin, axis=1, keepdims=True) + EPS)
    u = p0[...].astype(f32)
    for piece in (p1, p2, p3):
        u = u + piece[...].astype(f32)
    u = u * misc_ref[16:17, :].astype(f32)
    out = dresid_ref[...] + rinv * u - xin * (rinv * rinv * rinv) * jnp.mean(u * xin, axis=1, keepdims=True)
    out_ref[...] = out.astype(bf16)


def kernel_block_out(gx_ref, resid_ref, *rest):
    pieces, out_ref = rest[:2], rest[2]
    valid_row = jnp.broadcast_to((gx_ref[TOK + 8 : TOK + 9, :TOK].astype(f32) > 0.5).astype(f32), (TOK, TOK))
    valid = valid_row.T[:, 0:1]
    total = resid_ref[...]
    for piece in pieces:
        total = total + piece[...].astype(f32)
    out_ref[...] = (total * valid).astype(bf16)


def call(body, outs, ins, scratch=(), mib=60, flops=0, nbytes=0, name=None):
    return pl.pallas_call(
        body,
        out_shape=[jax.ShapeDtypeStruct(shape, dtype) for shape, dtype, _ in outs],
        in_specs=[spec for _, spec in ins],
        out_specs=[spec for _, _, spec in outs],
        scratch_shapes=list(scratch),
        compiler_params=params(mib),
        cost_estimate=pl.CostEstimate(flops=flops // 10**4, bytes_accessed=nbytes // 10**4, transcendentals=0),
        name=name,
    )(*[value for value, _ in ins])


def pick(value, axis, index):
    return lax.dynamic_index_in_dim(value, index, axis, keepdims=False)


def on_device(
    tokens, segment_ids, routes, cotangent, attn_gain, query_weight, key_weight, value_weight,
    output_weight, expert_gain, router_weight, expert_in, expert_out,
):
    V, A, S = spec_vmem(), spec_any(), spec_smem()
    iz, ih, ix, ic, il = [lax.axis_index(name) for name in AX]
    where = jnp.stack([iz, ih, ix, ic, il]).astype(jnp.int32)
    cos_np, sin_np = rope_tables()
    cos_full, sin_full = jnp.asarray(cos_np), jnp.asarray(sin_np)

    ints = jnp.concatenate(
        [routes.reshape(TOK, TOPK).T, segment_ids.reshape(1, TOK), jnp.zeros((7, TOK), jnp.int32)], axis=0
    ).astype(bf16)
    ints = jnp.pad(ints, ((0, 0), (0, D - TOK)))
    x_one = jnp.concatenate([tokens.reshape(TOK, D), ints], axis=0)
    g_own = jnp.concatenate([cotangent.reshape(TOK, D), ints], axis=0)
    small = jnp.concatenate(
        [router_weight, attn_gain[:, None], expert_gain[:, None], jnp.zeros((12, 46), bf16)], axis=1
    )
    heads = jnp.concatenate(
        [
            query_weight.reshape(12, 8, 192),
            key_weight.reshape(12, 8, 64),
            value_weight.reshape(12, 8, 64),
            jnp.broadcast_to(small[:, None, :], (12, 8, 64)),
        ],
        axis=2,
    ).transpose(1, 0, 2)
    heads = jnp.broadcast_to(heads[:, None], (8, 2, 12, QKVM)).reshape(16, 12, QKVM)
    heads = lax.all_to_all(heads, ("z", "c", "yl"), split_axis=0, concat_axis=0, tiled=True)
    heads = heads.reshape(4, 48, QKVM)
    o_in = jnp.stack(
        [output_weight, send(output_weight, dl=1), send(output_weight, dc=1), send(output_weight, dc=1, dl=1)]
    )
    o48 = jnp.take(o_in, (ic * 2 + il) ^ jnp.arange(4), axis=0, mode="clip").reshape(48, D)
    heads, o48, expert_in, x_first = lax.optimization_barrier((heads, o48, expert_in, x_one))
    x_own = jnp.stack([x_first] + [send(x_first, dz=j) for j in (1, 2, 3)])
    o48 = jnp.pad(o48.reshape(48, 6, 256), ((0, 0), (0, 2), (0, 0))).transpose(1, 0, 2)
    both = jnp.concatenate([heads, o48[:4], o48[4:]], axis=2)
    other = send(both, dh=1, dl=1)
    e_out = expert_out.reshape(8, 8, 3, 512).transpose(0, 2, 1, 3).reshape(8, 24, 512)
    e_pack = jnp.concatenate([expert_in, e_out], axis=2)
    e_pack = lax.all_to_all(e_pack, ("x", "c"), split_axis=0, concat_axis=0, tiled=True)
    g_y = jnp.stack([g_own, send(g_own, dl=1)])
    other, e_pack, x_own, g_y = lax.optimization_barrier((other, e_pack, x_own, g_y))
    o_mine = jnp.where(ih == ic, both[:, :, QKVM:], other[:, :, QKVM:])
    both = jnp.stack(
        [
            jnp.concatenate([both[:, :, :QKVM], o_mine[:, :, :256]], axis=2),
            jnp.concatenate([other[:, :, :QKVM], o_mine[:, :, 256:]], axis=2),
        ]
    )
    w_pieces = [both] + [send(both, dx=k) for k in (1, 2, 3)]
    dense = [(p, A) for p in w_pieces]
    x_sib = send(x_own, dc=1)
    x_all = [(x_own, V), (x_sib, V)]

    g_y, _ = lax.optimization_barrier((g_y, w_pieces))
    g_xy = [g_y] + [send(g_y, dx=k) for k in (1, 2, 3)]

    e_out = e_pack[:, :, 1024:].reshape(8, 3, 8, 512).transpose(1, 0, 2, 3).reshape(192, 512)
    e_pack = jnp.concatenate([e_pack[:, :, :1024].reshape(192, 1024), e_out], axis=1)
    e_full = lax.all_gather(e_pack, ("z", "yh"), axis=0, tiled=True)

    normed, qk_b, v_b, mixed, misc, part_own, part_sib = call(
        kernel_attn,
        [
            ((ROWS, D), bf16, A), ((ROWS, QK), bf16, V), ((ROWS, 128), bf16, V), ((ROWS, HQ), bf16, V),
            ((64, D), bf16, V), ((4, TOK, D), f32, A), ((4, TOK, D), bf16, A),
        ],
        [(where, S), (cos_full, V), (sin_full, V)] + x_all + dense,
        [
            pltpu.VMEM((D, QKVM), bf16), pltpu.VMEM((HQ, D), bf16), pltpu.VMEM((ROWS, D), bf16),
            pltpu.VMEM((4, TOK, D), f32), pltpu.VMEM((4, TOK, D), bf16),
            pltpu.SemaphoreType.DMA((32,)), pltpu.SemaphoreType.DMA((24,)), pltpu.SemaphoreType.DMA((9,)),
        ],
        flops=2 * ROWS * D * 512, nbytes=12 * 2**20, name="attention",
    )

    def core_sum(own, sib):
        return call(
            kernel_core_sum, [((TOK, D), bf16, V)] * 4, [(own, V), (send(sib, dc=1), V)],
            flops=10**6, nbytes=6 * 2**20, name="core_sum",
        )

    def team_sum(parts):
        return [parts[0]] + [send(parts[j], dz=j) for j in (1, 2, 3)]

    (attn_parts,) = call(
        kernel_core_sum_z, [((4, TOK, D), bf16, V)], [(where, S), (part_own, V), (send(part_sib, dc=1), V)],
        flops=10**6, nbytes=6 * 2**20, name="core_sum",
    )
    attn_parts = lax.all_to_all(attn_parts, "z", split_axis=0, concat_axis=0, tiled=True)
    resid, n2, gates, n2_a, n2_b = call(
        kernel_resid,
        [
            ((TOK, D), f32, V), ((TOK, D), bf16, V), ((16, TOK), f32, V),
            ((8, SEQ, D), bf16, V), ((8, SEQ, D), bf16, V),
        ],
        [(x_one, V), (attn_parts, V), (misc, V)],
        flops=10**7, nbytes=6 * 2**20, name="residual_norm",
    )

    def group_exchange(value):
        return lax.all_to_all(value, ("x", "yl"), split_axis=0, concat_axis=0, tiled=True)

    dn, mix, kept = [], [], []
    g_all = g_xy + [send(item, dc=1) for item in g_xy]
    group_rows = [group_exchange(n2_a), group_exchange(n2_b)]
    group_rows[0], g_all = lax.optimization_barrier((group_rows[0], g_all))
    for half, rows in enumerate(group_rows):
        if half:
            rows, _ = lax.optimization_barrier((rows, outs[0]))
        rows_sib = send(rows, dc=1)
        outs = call(
            functools.partial(kernel_expert, half),
            [
                ((8, 80, D), bf16, A), ((8, SEQ, D), bf16, A),
                ((512, D), bf16, A), ((512, D), bf16, A), ((512, F), bf16, A), ((512, 1024), bf16, A),
            ]
            + [((2, 80, D), bf16, A)] * 4
            + [((8, SEQ, D), bf16, A)],
            [(where, S), (misc, V), (rows, A), (rows_sib, A), (e_full, A)] + [(p, A) for p in g_all],
            [
                pltpu.VMEM((16, SEQ, D), bf16), pltpu.VMEM((16, 80, D), bf16),
                pltpu.VMEM((D, 1024), bf16), pltpu.VMEM((F, D), bf16),
                pltpu.VMEM((16, SEQ), f32), pltpu.VMEM((16, SEQ), f32), pltpu.VMEM((16, 1024), f32),
                pltpu.VMEM((512, D), bf16), pltpu.VMEM((512, D), bf16), pltpu.VMEM((512, F), bf16),
                pltpu.VMEM((512, 1024), bf16), pltpu.VMEM((16, 80, D), bf16), pltpu.VMEM((16, SEQ, D), bf16),
                pltpu.SemaphoreType.DMA((2,)), pltpu.SemaphoreType.DMA((32,)), pltpu.SemaphoreType.DMA((32,)),
                pltpu.SemaphoreType.DMA((18,)),
            ],
            flops=6 * 10**9, nbytes=30 * 2**20, name="experts",
        )
        recv = [send(v, dc=1) for v in outs[6:10]]
        if half:
            recv, dn[0] = lax.optimization_barrier((recv, dn[0]))
        (summed,) = call(
            kernel_pair_sum, [((8, 80, D), bf16, V)], [(outs[0], V)] + [(v, V) for v in recv],
            flops=10**7, nbytes=6 * 2**20, name="pair_sum",
        )
        dn.append(group_exchange(summed))
        mix.append((outs[1], outs[10]))
        kept.extend(outs[2:6])
    kept[0], _ = lax.optimization_barrier((kept[0], summed))
    (e_grad,) = call(
        kernel_expert_grads, [((D, D), bf16, V)], [(v, V) for v in kept],
        flops=6 * 10**9, nbytes=14 * 2**20, name="expert_gradients",
    )
    mix[1], _ = lax.optimization_barrier((mix[1], e_grad))
    mix_in = [(v, V) for own, sib in mix for v in (own, send(sib, dc=1))]
    mix_sum = call(
        kernel_mix_sum, [((2, SEQ, D), bf16, V)] * 8, [(where, S)] + mix_in,
        flops=10**7, nbytes=10 * 2**20, name="mix_sum",
    )
    dn[1], e_grad, mix_sum = lax.optimization_barrier((dn[1], e_grad, mix_sum))
    dresid, dattn, small_grad = call(
        kernel_home,
        [((TOK, D), f32, V), ((4, TOK, D), bf16, V), ((32, D), f32, V)],
        [(g_own, V), (resid, V), (n2, V), (gates, V), (misc, V), (dn[0], V), (dn[1], V)],
        [pltpu.VMEM((16, TOK), f32)],
        flops=10**8, nbytes=6 * 2**20, name="home_gradient",
    )
    e_grad, dattn = lax.optimization_barrier((e_grad, dattn))
    e_sum = lax.psum_scatter(e_grad, ("z", "yh"), scatter_dimension=0, tiled=True)
    da_own = lax.all_to_all(dattn, "z", split_axis=0, concat_axis=0, tiled=True)
    mix_x = [[mix_sum[h4]] + [send(mix_sum[h4 + k], dx=k) for k in (1, 2, 3)] for h4 in (0, 4)]
    da_own, mix_x[0] = lax.optimization_barrier((da_own, mix_x[0]))
    da_all = [da_own, send(da_own, dc=1)]
    wg_out, dcat = call(
        kernel_back,
        [((4, 2, 4, 48, WIDE), bf16, A), ((ROWS, QKVM), bf16, V)],
        [
            (where, S), (normed, A), (qk_b, V), (v_b, V), (mixed, V), (small_grad, V), (cos_full, V), (sin_full, V),
            (x_own, A), (x_sib, A),
        ]
        + [(p, V) for p in da_all]
        + dense,
        [
            pltpu.VMEM((D, QKVM), bf16), pltpu.VMEM((HQ, D), bf16), pltpu.VMEM((ROWS, D), bf16),
            pltpu.VMEM((ROWS, HQ), bf16), pltpu.VMEM((ROWS, QK), f32),
            pltpu.VMEM((D, QKVM), bf16), pltpu.VMEM((HQ, D + 512), bf16), pltpu.VMEM((8, 16, TOK), bf16),
            pltpu.VMEM((ROWS, D), bf16),
            pltpu.SemaphoreType.DMA((32,)), pltpu.SemaphoreType.DMA((24,)), pltpu.SemaphoreType.DMA((64,)),
            pltpu.SemaphoreType.DMA((9,)),
        ],
        flops=6 * ROWS * D * 512, nbytes=20 * 2**20, name="attention_back",
    )
    wg_out, mix_x[1] = lax.optimization_barrier((wg_out, mix_x[1]))
    wg = lax.all_to_all(wg_out, "x", split_axis=0, concat_axis=0, tiled=True)
    mix_keep, mix_give = call(
        kernel_mix_pair, [((TOK, D), bf16, V)] * 2, [(where, S)] + [(p, V) for p in mix_x[0] + mix_x[1]],
        flops=10**6, nbytes=5 * 2**20, name="mix_pair",
    )
    dn1_own, dn1_sib = call(
        kernel_back_tokens,
        [((4, TOK, D), f32, V), ((4, TOK, D), bf16, V)],
        [(where, S), (dcat, V)] + dense,
        [pltpu.VMEM((D, QKVM), bf16), pltpu.SemaphoreType.DMA((32,))],
        flops=2 * ROWS * D * QKVM, nbytes=10 * 2**20, name="token_back",
    )
    wg, dn1_own, dn1_sib, mix_keep, mix_give = lax.optimization_barrier((wg, dn1_own, dn1_sib, mix_keep, mix_give))
    dn1_parts = core_sum(dn1_own, dn1_sib)
    (block_out,) = call(
        kernel_block_out, [((TOK, D), bf16, V)],
        [(g_own, V), (resid, V), (mix_keep, V), (send(mix_give, dl=1), V)],
        flops=10**7, nbytes=5 * 2**20, name="block_output",
    )
    dn1_pieces = team_sum(dn1_parts)
    keep, give = call(
        kernel_dense_sum, [((4, 48, QKVM + 384), bf16, V)] * 2, [(where, S), (wg, V)],
        flops=10**6, nbytes=5 * 2**20, name="dense_sum",
    )
    take = send(give, dh=1, dl=1)
    e_sum, _ = lax.optimization_barrier((e_sum, give))
    ge_out = e_sum[:, 1024:].reshape(3, 8, 8, 512).transpose(1, 0, 2, 3).reshape(8, 24, 512)
    ge = jnp.concatenate([e_sum[:, :1024].reshape(8, 24, 1024), ge_out], axis=2)
    ge = lax.all_to_all(ge, ("x", "c"), split_axis=0, concat_axis=0, tiled=True)
    keep = (keep.astype(f32) + take.astype(f32)).astype(bf16)
    keep, ge = lax.optimization_barrier((keep, ge))
    heads = keep[:, :, :QKVM].reshape(16, 12, QKVM)
    heads = lax.all_to_all(heads, ("z", "c", "yl"), split_axis=0, concat_axis=0, tiled=True)
    heads, dn1_pieces, keep = lax.optimization_barrier((heads, dn1_pieces, keep))
    (token_grad,) = call(
        kernel_token_grad, [((TOK, D), bf16, V)],
        [(x_one, V), (dresid, V)] + [(p, V) for p in dn1_pieces] + [(misc, V)],
        flops=10**7, nbytes=3 * 2**20, name="token_gradient",
    )
    back = keep[:, :, QKVM:].transpose(1, 0, 2).reshape(4, 12, D)
    me = ic * 2 + il
    d_o = pick(back, 0, me).astype(f32) + send(pick(back, 0, me ^ 1), dl=1).astype(f32)
    d_o = d_o + send(pick(back, 0, me ^ 2), dc=1).astype(f32) + send(pick(back, 0, me ^ 3), dc=1, dl=1).astype(f32)
    ge = ge.astype(f32)
    ge_in = ge[:, :, :1024]
    ge_out = ge[:, :, 1024:].reshape(8, 3, 8, 512).transpose(0, 2, 1, 3).reshape(8, 8, D)
    heads = heads.astype(f32).reshape(8, 2, 12, QKVM).sum(axis=1)
    dq = heads[:, :, :HQ].transpose(1, 0, 2).reshape(12, D)
    dk = heads[:, :, HQ:QK].transpose(1, 0, 2).reshape(12, 512)
    dv = heads[:, :, QK:QKV].transpose(1, 0, 2).reshape(12, 512)
    d_small = heads[:, :, QKV:].sum(axis=0)
    return (
        block_out.reshape(2, SEQ, D),
        token_grad.reshape(2, SEQ, D),
        d_small[:, 16],
        dq,
        dk,
        dv,
        d_o,
        d_small[:, 17],
        d_small[:, :16],
        ge_in,
        ge_out,
    )


def solution(mesh):
    devices = mesh.devices.reshape(DIMS) if hasattr(mesh, "devices") else None
    fine = Mesh(devices, AX)
    every = ("z", "yh", "x", "c", "yl")
    dp = ("z", "yh", "x", "c")
    in_specs = (
        P(every, None, None), P(every, None), P(every, None, None), P(every, None, None), P(every),
        P(every, None), P(every, None), P(every, None), P(every, None), P(every), P(every, None),
        P("yl", dp, None), P("yl", dp, None),
    )
    out_specs = (
        P(every, None, None), P(every, None, None), P(every), P(every, None), P(every, None),
        P(every, None), P(every, None), P(every), P(every, None), P("yl", dp, None), P("yl", dp, None),
    )
    return jax.shard_map(on_device, mesh=fine, in_specs=in_specs, out_specs=out_specs, check_vma=False)
```
